32 devices in a mesh: groups: 2 (over y), ep: 8 (over z, core), pd: 2 (over x).
Axes of the slice: x: 2, y: 2, z: 4, core: 2. Of those that a mesh axis runs over, the one named last changes fastest.
Arguments:
- hidden: bfloat16 [2048, 7168], P(('groups', 'ep', 'pd')), parts along dimension 0, may hold values from -6 to 6
- moe_gain: float32 [7168], replicated, may hold values from 0.4 to 1.6
- expert_ids: int32 [2048, 2], P(('groups', 'ep', 'pd')), parts along dimension 0, may hold values from 0 to 7, all different within a row; in each aligned block of 64 rows (0 to 63, 64 to 127, ...) at most 32 rows name the same one
- gate_scores: float32 [2048, 2], P(('groups', 'ep', 'pd')), parts along dimension 0, may hold values from 0.05 to 1
- gate_up: bfloat16 [8, 7168, 2, 1024], P('ep', None, None, 'pd'), may hold values from -0.0625 to 0.0625
- down_proj: bfloat16 [8, 1024, 7168], P('ep', 'pd'), may hold values from -0.1875 to 0.1875
- kv_weight: bfloat16 [7168, 576], P('ep'), may hold values from -0.0625 to 0.0625
- attn_gain: float32 [7168], replicated, may hold values from 0.4 to 1.6
- kv_gain: float32 [512], replicated, may hold values from 0.25 to 1.75
- prompt_lens: int32 [32], P('groups'), parts along dimension 0, may hold values from 1 to 192, 1024 in all
- assign: int32 [32], P('groups'), parts along dimension 0, may hold values from 0 to 15, each once
- latent_cache: bfloat16 [32, 512, 576], P(('groups', 'ep', 'pd')), parts along dimension 0, may hold values from -17 to 17
- cache_len: int32 [32], P(('groups', 'ep', 'pd')), parts along dimension 0, may hold values from 1 to 512, 4096 in all
- draft_hidden: bfloat16 [32, 4, 7168], P(('groups', 'ep', 'pd')), parts along dimension 0, may hold values from -6 to 6
- queries: bfloat16 [32, 4, 64, 576], P(('groups', 'ep', 'pd')), parts along dimension 0, may hold values from -140 to 140
Outputs:
- layer_out: bfloat16 [2048, 7168], P(('groups', 'ep', 'pd')), parts along dimension 0
- decoded: bfloat16 [32, 4, 64, 512], P(('groups', 'ep', 'pd')), parts along dimension 0
The draws below stay inside these ranges and needn't reach their ends.
There are 2 independent parts, one for each index of `groups`. The reference program is written for one: setup_inputs(seed, part) draws one part's arguments, and reference() takes and returns one part's arrays. A program takes and returns all parts, laid end to end along the dimension named above; an argument that names none is the same for every part. Nothing has to cross between parts.
Inputs may be any that keep to these rules, and one draw needn't show every extreme that they name: `expert_ids`: each row names 2 different experts. Among the rows of one device (64 tokens) no expert is named more than 32 times, a bound that some block reaches. `prompt_lens`: the blocks lie end to end over all 1024 token rows, in order; the longest has 192 rows. `assign`: every slot receives exactly one prompt block. `cache_len`: some slot is full.
All inputs are finite; a program needn't handle non-finite values. No bound on the sum of `cache_len` on one device may be relied on, other than what follows from the above.
Results may differ from the reference program's by a relative error of at most 0.0086.
Values may be sent and summed in bfloat16 or wider, within the bound.
A program may use at most 128 MiB of HBM per device.

```python
import math
import jax
import jax.numpy as jnp
import numpy as np
from jax import lax

D = 7168
FF = 1024
LAT = 512
ROPE = 64
HEADS = 64
TOPK = 2
STEPS = 4
TOK_DEV = 64
CACHE = 512
KV = 576
EXPERTS = 8
TOKENS = 1024
PROMPTS = 16
CAP = 32
MOST = 192
N_PD = 2


def rough_cache(key):
    base = jnp.clip(jax.random.normal(jax.random.fold_in(key, 11), (PROMPTS, CACHE, KV), jnp.float32), -6.0, 6.0)
    return base


def draw_latent_cache(key, part):
    return rough_cache(key).astype(jnp.bfloat16)


def draw_queries(key, part):
    power_low = 0.0
    cache_rows = rough_cache(key)
    key = jax.random.fold_in(key, 5)
    base = jnp.clip(jax.random.normal(jax.random.fold_in(key, 1), (PROMPTS, STEPS, HEADS, KV), jnp.float32), -6.0, 6.0)
    chosen = jax.random.uniform(jax.random.fold_in(key, 2), (PROMPTS, STEPS, HEADS), jnp.float32) < 0.125
    power = power_low * jax.random.uniform(jax.random.fold_in(key, 3), (PROMPTS, STEPS, HEADS), jnp.float32, 1.0, 2.7)
    first_rows = cache_rows[:, 0, :LAT][:, None, None, :]
    aligned = jnp.concatenate([power[..., None] * first_rows, base[..., LAT:]], axis=-1)
    chosen = chosen & (power > 0.0)
    return jnp.where(chosen[..., None], aligned, base).astype(jnp.bfloat16)


def block_scale(own_key, shape, cuts, low, largest):
    level = 1.0
    for axis_at, blocks in cuts:
        steps = jax.random.uniform(jax.random.fold_in(jax.random.fold_in(own_key, 6), axis_at), (blocks,), jnp.float32, low / len(cuts), largest / len(cuts))
        level = level * jnp.repeat(jnp.exp(steps), shape[axis_at] // blocks).reshape((-1,) + (1,) * (len(shape) - 1 - axis_at))
    return level


def length_profile(number_of, total, reach, lean):
    loads = [(1 << 20) // math.isqrt(standing ** lean) + 1 for standing in range(2, number_of + 1)]
    spare, given = total - reach - (number_of - 1), [1] * (number_of - 1)
    while spare > 0:
        candidates = [i for i in range(number_of - 1) if given[i] < reach]
        mass, left = sum([loads[i] for i in candidates]), spare
        for i in candidates:
            more = min(reach - given[i], max(1, left * loads[i] // mass), spare)
            given[i] = given[i] + more
            spare = spare - more
    return np.array([reach] + given)


def ragged(rng, amount, total, limit, skew):
    if amount == 2:
        one = jax.random.randint(rng, (), max(1, total - limit), min(limit, total - 1) + 1)
        return jnp.stack([one, total - one])
    lengths = jnp.asarray(length_profile(amount, total, limit, skew), jnp.int32)
    couples = (amount - 1) // 2
    source_of, taker = lengths[1:1 + 2 * couples:2], lengths[2:2 + 2 * couples:2]
    slack = jnp.minimum(source_of - 1, limit - taker)
    passed = jax.random.randint(jax.random.fold_in(rng, 1), (couples,), 0, 1 << 20) % (slack + 1)
    lengths = lengths.at[1:1 + 2 * couples:2].set(source_of - passed).at[2:2 + 2 * couples:2].set(taker + passed)
    return lengths[jax.random.permutation(jax.random.fold_in(rng, 2), amount)]


def shared_out(rng, own, number, rows, count, top, reach, skew):
    ranking = jax.random.permutation(rng, count)
    packed, common = load_shares(count, rows * top, reach, skew, True), load_shares(count, rows * top, reach, skew, False)
    places = jnp.arange(count)

    def named(tallies, offset_by):
        used = int((tallies > 0).sum())
        fixed = max(1, used // 4)
        moved = fixed + (places - fixed + offset_by * (used - fixed)) % max(1, count - fixed)
        return jnp.zeros((count,), jnp.int32).at[ranking[jnp.where(places < fixed, places, moved)]].set(jnp.asarray(tallies, jnp.int32))

    tallies = jnp.where(number % 4 == 0, named(packed, number // 4), named(common, number - number // 4 - 1))
    mixed = jax.random.permutation(jax.random.fold_in(own, 3), count)
    donor, receiver = mixed[0:count // 2 * 2:2], mixed[1:count // 2 * 2:2]
    margin = jnp.minimum(tallies[donor] - 1, reach - tallies[receiver]) // 2
    margin = jnp.where((donor == ranking[0]) | (receiver == ranking[0]) | (tallies[receiver] == 0), 0, jnp.maximum(margin, 0))
    moved = jax.random.randint(jax.random.fold_in(own, 4), (count // 2,), 0, 1 << 20) % (margin + 1)
    tallies = tallies.at[donor].add(-moved).at[receiver].add(moved)
    labels = jnp.searchsorted(jnp.cumsum(tallies), jnp.arange(rows * top), side="right").astype(jnp.int32)
    listing = labels.reshape(top, rows).T
    listing = listing[jax.random.permutation(jax.random.fold_in(own, 1), rows)]
    offset_by = jax.random.randint(jax.random.fold_in(own, 2), (rows, 1), 0, top)
    return jnp.take_along_axis(listing, (jnp.arange(top)[None, :] + offset_by) % top, axis=1)


def load_shares(count, total, reach, skew, full):
    weights = [(1 << 20) // math.isqrt(rank ** skew) + 1 for rank in range(1, count + 1)]
    largest = reach if full else min(reach, max(-(-total // count), total * weights[0] // sum(weights)))
    least = 1 if total - largest >= count - 1 else 0
    holding, spare = [largest] + [least] * (count - 1), total - largest - least * (count - 1)
    while spare > 0:
        free = [i for i in range(1, count) if holding[i] < largest] or [i for i in range(1, count) if holding[i] < reach]
        whole, budget = sum([weights[i] for i in free]), spare
        for i in free:
            addition = min(reach - holding[i], max(1, budget * weights[i] // whole), spare)
            holding[i] = holding[i] + addition
            spare = spare - addition
    return np.array(holding)


def noise(key, extent, width, bound, pieces=(), held_as=jnp.bfloat16):
    factor_of = block_scale(key, extent, pieces, -0.22, 0.18) if pieces else 1.0
    array = jax.random.normal(key, extent, jnp.float32) * width * factor_of
    return jnp.minimum(jnp.maximum(array, -bound), bound).astype(held_as)


def setup_inputs(seed: int = 0, part: int = 0) -> dict:
    keys = jax.random.split(jax.random.key(seed), 16)
    part_splits = jax.random.split(jax.random.fold_in(keys[15], part), 16)
    hidden = noise(part_splits[0], (TOKENS, D), 1.0, 6.0, ((0, 16),))
    moe_gain = jnp.clip(1.0 + 0.12 * jax.random.normal(keys[1], (D,), jnp.float32), 0.4, 1.6)
    expert_ids_keys = jax.random.split(jax.random.fold_in(part_splits[2], 1), TOKENS // TOK_DEV)
    expert_ids_turns = jax.random.permutation(jax.random.fold_in(part_splits[2], 3), TOKENS // TOK_DEV)
    expert_ids = jax.vmap(lambda own, number: shared_out(jax.random.fold_in(part_splits[2], 2), own, number, TOK_DEV, EXPERTS, TOPK, CAP, 2))(expert_ids_keys, expert_ids_turns).reshape((TOKENS, TOPK))
    gate_scores = jnp.clip(0.05 + 0.95 * jax.random.uniform(part_splits[3], (TOKENS, TOPK), jnp.float32) ** block_scale(part_splits[3], (TOKENS, TOPK), ((0, 16),), -0.2, 0.2), 0.05, 1.0)
    gate_up = noise(keys[4], (EXPERTS, D, 2, FF), D ** -0.5, 0.0625, ((0, 8), (3, 2)))
    down_proj = noise(keys[5], (EXPERTS, FF, D), FF ** -0.5, 0.1875, ((0, 8), (1, 2)))
    kv_weight = noise(keys[6], (D, KV), D ** -0.5, 0.0625, ((0, 8),))
    attn_gain = jnp.clip(1.0 + 0.12 * jax.random.normal(keys[7], (D,), jnp.float32), 0.4, 1.6)
    kv_gain = jnp.clip(1.0 + 0.15 * jax.random.normal(keys[8], (LAT,), jnp.float32), 0.25, 1.75)
    prompt_lens = ragged(part_splits[9], PROMPTS, TOKENS, MOST, 2).astype(jnp.int32)
    assign = jax.random.permutation(part_splits[10], PROMPTS).astype(jnp.int32)
    latent_cache = draw_latent_cache(jax.random.fold_in(jax.random.fold_in(keys[15], part), 71), part)
    cache_len = ragged(part_splits[12], PROMPTS, PROMPTS * CACHE // 2, CACHE, 1).astype(jnp.int32)
    draft_hidden = noise(part_splits[13], (PROMPTS, STEPS, D), 1.0, 6.0, ((0, 16),))
    queries = draw_queries(jax.random.fold_in(jax.random.fold_in(keys[15], part), 71), part)
    return dict(hidden=hidden, moe_gain=moe_gain, expert_ids=expert_ids, gate_scores=gate_scores, gate_up=gate_up, down_proj=down_proj, kv_weight=kv_weight, attn_gain=attn_gain, kv_gain=kv_gain, prompt_lens=prompt_lens, assign=assign, latent_cache=latent_cache, cache_len=cache_len, draft_hidden=draft_hidden, queries=queries)


NORM_EPSILON = 1e-06
ROUTE_SCALE = 2.5
SCORE_SCALE = 192.0 ** (-0.5)
ROPE_BASE = 10000.0

def rms_norm(values, gain):
    return values * lax.rsqrt(lax.optimization_barrier(jnp.mean(values * values, axis=-1, keepdims=True)) + NORM_EPSILON) * gain

def with_rope(row_vals, positions):
    latent_width = row_vals.shape[-1] - ROPE
    rotary = row_vals[..., latent_width:].astype(jnp.float32)
    frequency = ROPE_BASE ** (-jnp.arange(ROPE // 2, dtype=jnp.float32) * 2.0 / ROPE)
    angles = positions.astype(jnp.float32)[..., None] * frequency
    even_part = rotary[..., 0::2]
    odd_part = rotary[..., 1::2]
    turned = jnp.stack([even_part * jnp.cos(angles) - odd_part * jnp.sin(angles), even_part * jnp.sin(angles) + odd_part * jnp.cos(angles)], axis=-1).reshape(rotary.shape)
    return jnp.concatenate([row_vals[..., :latent_width], turned.astype(jnp.bfloat16)], axis=-1)

def latent_rows(acts, norm_gain, kv_weight, kv_gain):
    normed = rms_norm(acts.astype(jnp.float32), norm_gain).astype(jnp.bfloat16)
    compressed = jnp.dot(normed, kv_weight, preferred_element_type=jnp.float32)
    latent_part = rms_norm(compressed[:, :LAT], kv_gain)
    return jnp.concatenate([latent_part, compressed[:, LAT:]], axis=-1).astype(jnp.bfloat16)

def slot_attention(query, cache_rows, block_rows, draft_rows, cached, block_len):
    step_count = query.shape[0]
    block_cap = block_rows.shape[0]
    cache_cap = cache_rows.shape[0]
    block_pos = cached + jnp.arange(block_cap, dtype=jnp.int32)
    draft_pos = cached + block_len + jnp.arange(step_count, dtype=jnp.int32)
    key_rows = jnp.concatenate([cache_rows, with_rope(block_rows, block_pos), with_rope(draft_rows, draft_pos)], axis=0)
    head_pos = jnp.broadcast_to(draft_pos[:, None], query.shape[:2])
    turned_query = with_rope(query, head_pos)
    live_cache = jnp.broadcast_to((jnp.arange(cache_cap, dtype=jnp.int32) < cached)[None, :], (step_count, cache_cap))
    live_block = jnp.broadcast_to((jnp.arange(block_cap, dtype=jnp.int32) < block_len)[None, :], (step_count, block_cap))
    step_ids = jnp.arange(step_count, dtype=jnp.int32)
    live_draft = step_ids[None, :] <= step_ids[:, None]
    live_rows = jnp.concatenate([live_cache, live_block, live_draft], axis=1)
    scores = jnp.einsum('thk,nk->thn', turned_query.astype(jnp.float32), key_rows.astype(jnp.float32)) * SCORE_SCALE
    scores = jnp.where(live_rows[:, None, :], scores, -1e+30)
    peak = lax.optimization_barrier(jnp.max(scores, axis=-1, keepdims=True))
    expo = jnp.exp(scores - peak)
    weights = (expo / lax.optimization_barrier(jnp.sum(expo, axis=-1, keepdims=True))).astype(jnp.bfloat16)
    output = jnp.einsum('thn,nl->thl', weights.astype(jnp.float32), key_rows[:, :LAT].astype(jnp.float32))
    return output.astype(jnp.bfloat16)

def reference(hidden, moe_gain, expert_ids, gate_scores, gate_up, down_proj, kv_weight, attn_gain, kv_gain, prompt_lens, assign, latent_cache, cache_len, draft_hidden, queries):
    block_count = TOKENS // TOK_DEV
    routed = TOK_DEV * TOPK
    part_width = FF // N_PD
    normed = rms_norm(hidden.astype(jnp.float32), moe_gain).astype(jnp.bfloat16)
    route_weight = ROUTE_SCALE * gate_scores / lax.optimization_barrier(jnp.sum(gate_scores, axis=-1, keepdims=True))
    flat_ids = expert_ids.reshape(block_count, routed)
    one_hot = (flat_ids[..., None] == jnp.arange(EXPERTS, dtype=jnp.int32)).astype(jnp.int32)
    slot_rank = lax.optimization_barrier(jnp.sum(one_hot * (jnp.cumsum(one_hot, axis=1, dtype=jnp.int32) - 1), axis=-1, dtype=jnp.int32))
    token_rows = normed.reshape(block_count, TOK_DEV, D)
    weight_rows = route_weight.reshape(block_count, routed)
    routed_ids = jnp.arange(routed, dtype=jnp.int32)

    def one_expert(running, expert):
        hit = (flat_ids == expert)[:, None, :] & (slot_rank[:, None, :] == jnp.arange(CAP, dtype=jnp.int32)[None, :, None])
        valid = jnp.any(hit, axis=-1)
        picked = lax.optimization_barrier(jnp.sum(jnp.where(hit, routed_ids, 0), axis=-1, dtype=jnp.int32))
        token_idx = (picked // TOPK).astype(jnp.int32)
        gathered = jax.vmap(lambda rows_b, idx_b: rows_b[idx_b])(token_rows, token_idx).reshape(-1, D)
        gate_val = jnp.einsum('rd,dgf->rgf', gathered.astype(jnp.float32), gate_up[expert].astype(jnp.float32))
        activated = (jax.nn.silu(gate_val[:, 0]) * gate_val[:, 1]).astype(jnp.bfloat16)
        expert_down = down_proj[expert]
        summed = jnp.zeros((gathered.shape[0], D), jnp.float32)
        for quarter in range(N_PD):
            partial_value = jnp.dot(activated[:, quarter * part_width:(quarter + 1) * part_width], expert_down[quarter * part_width:(quarter + 1) * part_width], preferred_element_type=jnp.float32).astype(jnp.bfloat16)
            partial_value = lax.optimization_barrier(partial_value)
            summed = summed + partial_value.astype(jnp.float32)
        expert_out = summed.astype(jnp.bfloat16).reshape(block_count, CAP, D)
        factor = lax.optimization_barrier(jnp.sum(jnp.where(hit, weight_rows[:, None, :], 0.0), axis=-1)) * valid.astype(jnp.float32)
        contrib = expert_out.astype(jnp.float32) * factor[..., None]
        running = jax.vmap(lambda acc_b, idx_b, add_b: acc_b.at[idx_b].add(add_b))(running, token_idx, contrib)
        return (running, None)
    mixture, _ = lax.scan(one_expert, jnp.zeros((block_count, TOK_DEV, D), jnp.float32), jnp.arange(EXPERTS, dtype=jnp.int32))
    layer_out = (hidden.astype(jnp.float32) + mixture.reshape(TOKENS, D)).astype(jnp.bfloat16)
    prompt_latent = latent_rows(layer_out, attn_gain, kv_weight, kv_gain)
    draft_latent = latent_rows(draft_hidden.reshape(-1, D), attn_gain, kv_weight, kv_gain).reshape(PROMPTS, STEPS, KV)
    owner_prompt = jnp.zeros((PROMPTS,), jnp.int32).at[assign].set(jnp.arange(PROMPTS, dtype=jnp.int32))
    starts = (jnp.cumsum(prompt_lens, dtype=jnp.int32) - prompt_lens).astype(jnp.int32)
    padded = jnp.concatenate([prompt_latent, jnp.zeros((MOST, KV), jnp.bfloat16)], axis=0)

    def one_slot(slot_id):
        prompt = owner_prompt[slot_id]
        block_len = prompt_lens[prompt]
        block_rows = lax.dynamic_slice_in_dim(padded, starts[prompt].astype(jnp.int32), MOST, 0)
        block_rows = jnp.where((jnp.arange(MOST, dtype=jnp.int32) < block_len)[:, None], block_rows, jnp.zeros_like(block_rows))
        return slot_attention(queries[slot_id], latent_cache[slot_id], block_rows, draft_latent[slot_id], cache_len[slot_id], block_len)
    decoded = lax.map(one_slot, jnp.arange(PROMPTS, dtype=jnp.int32))
    return (layer_out, decoded)
```

```python
import functools

import jax
import jax.numpy as jnp
from jax import lax
from jax.experimental import pallas as pl
from jax.experimental.pallas import tpu as pltpu
from jax.sharding import PartitionSpec as P

NORM_EPSILON = 1e-06
ROUTE_SCALE = 2.5
SCORE_SCALE = 192.0 ** (-0.5)
ROPE_BASE = 10000.0


def rms_norm(values, gain):
    return (
        values * lax.rsqrt(jnp.mean(values * values, axis=-1, keepdims=True) + NORM_EPSILON) * gain
    )


def with_rope(row_vals, positions, rotary_width):
    latent_width = row_vals.shape[-1] - rotary_width
    rotary = row_vals[..., latent_width:].astype(jnp.float32)
    frequency = ROPE_BASE ** (
        -jnp.arange(rotary_width // 2, dtype=jnp.float32) * 2.0 / rotary_width
    )
    angles = positions.astype(jnp.float32)[..., None] * frequency
    even_part = rotary[..., 0::2]
    odd_part = rotary[..., 1::2]
    turned = jnp.stack(
        [
            even_part * jnp.cos(angles) - odd_part * jnp.sin(angles),
            even_part * jnp.sin(angles) + odd_part * jnp.cos(angles),
        ],
        axis=-1,
    ).reshape(rotary.shape)
    return jnp.concatenate([row_vals[..., :latent_width], turned.astype(jnp.bfloat16)], axis=-1)


def slot_attention(query, cache_rows, block_rows, draft_rows, cached, block_len, latent_width):
    step_count, head_count, row_width = query.shape
    rotary_width = row_width - latent_width
    block_cap = block_rows.shape[0]
    cache_cap = cache_rows.shape[0]
    block_pos = cached + jnp.arange(block_cap, dtype=jnp.int32)
    draft_pos = cached + block_len + jnp.arange(step_count, dtype=jnp.int32)
    key_rows = jnp.concatenate(
        [
            cache_rows,
            with_rope(block_rows, block_pos, rotary_width),
            with_rope(draft_rows, draft_pos, rotary_width),
        ],
        axis=0,
    )
    head_pos = jnp.broadcast_to(draft_pos[:, None], (step_count, head_count))
    turned_query = with_rope(query, head_pos, rotary_width).reshape(
        step_count * head_count, row_width
    )
    live_cache = jnp.broadcast_to(
        (jnp.arange(cache_cap, dtype=jnp.int32) < cached)[None, :], (step_count, cache_cap)
    )
    live_block = jnp.broadcast_to(
        (jnp.arange(block_cap, dtype=jnp.int32) < block_len)[None, :], (step_count, block_cap)
    )
    step_ids = jnp.arange(step_count, dtype=jnp.int32)
    live_draft = step_ids[None, :] <= step_ids[:, None]
    live_rows = jnp.concatenate([live_cache, live_block, live_draft], axis=1)
    scores = (
        jnp.einsum("qk,nk->qn", turned_query, key_rows, preferred_element_type=jnp.float32)
        * SCORE_SCALE
    )
    scores = scores.reshape(step_count, head_count, -1)
    scores = jnp.where(live_rows[:, None, :], scores, -1e30)
    peak = jnp.max(scores, axis=-1, keepdims=True)
    expo = jnp.exp(scores - peak)
    weights = (expo / jnp.sum(expo, axis=-1, keepdims=True)).astype(jnp.bfloat16)
    output = jnp.dot(
        weights.reshape(step_count * head_count, -1),
        key_rows[:, :latent_width],
        preferred_element_type=jnp.float32,
    )
    return output.reshape(step_count, head_count, latent_width).astype(jnp.bfloat16)


def peer_order(count):
    order = []
    far, near = count // 2, 1
    for distance in (far, near, count - 1):
        if 0 < distance < count and distance not in order:
            order.append(distance)
    for distance in range(1, count):
        if distance not in order:
            order.append(distance)
    return order


def meet_peers(ep_size, pd_size):
    me, column = lax.axis_index("ep"), lax.axis_index("pd")
    barrier = pltpu.get_barrier_semaphore()
    for distance in range(1, ep_size):
        pl.semaphore_signal(
            barrier,
            inc=1,
            device_id={"ep": lax.rem(me + distance, ep_size)},
            device_id_type=pl.DeviceIdType.MESH,
        )
    for distance in range(1, pd_size):
        pl.semaphore_signal(
            barrier,
            inc=1,
            device_id={"pd": lax.rem(column + distance, pd_size)},
            device_id_type=pl.DeviceIdType.MESH,
        )
    pl.semaphore_wait(barrier, ep_size - 1 + pd_size - 1)


def spread_kernel(
    ep_size, pd_size, shared, pieces, src, out, local_sem, send_sem, recv_sem, pass_sem, got_sem
):
    me, column = lax.axis_index("ep"), lax.axis_index("pd")
    width = out.shape[-1] // pieces
    order = peer_order(ep_size)
    meet_peers(ep_size, pd_size)

    def part(ref, piece):
        return ref if pieces == 1 else ref.at[:, pl.ds(piece * width, width)]

    def block(target):
        return src if shared else src.at[target]

    def direct(distance, piece):
        target = lax.rem(me + distance, ep_size)
        return pltpu.make_async_remote_copy(
            src_ref=part(block(target), piece),
            dst_ref=part(out.at[column, me], piece),
            send_sem=send_sem.at[distance, piece],
            recv_sem=recv_sem.at[distance, piece],
            device_id={"ep": target},
            device_id_type=pl.DeviceIdType.MESH,
        )

    def across(owner, from_src, step, distance, piece):
        whole = block(me) if from_src else out.at[column, owner]
        return pltpu.make_async_remote_copy(
            src_ref=part(whole, piece),
            dst_ref=part(out.at[column, owner], piece),
            send_sem=pass_sem.at[step, distance, piece],
            recv_sem=got_sem.at[step, distance, piece],
            device_id={"pd": lax.rem(column + step, pd_size)},
            device_id_type=pl.DeviceIdType.MESH,
        )

    own = pltpu.make_async_copy(block(me), out.at[column, me], local_sem)
    own.start()
    for piece in range(pieces):
        for step in range(1, pd_size):
            across(me, True, step, 0, piece).start()
    for distance in order:
        for piece in range(pieces):
            direct(distance, piece).start()
    for distance in order:
        for piece in range(pieces):
            owner = lax.rem(me - distance + ep_size, ep_size)
            direct(distance, piece).wait_recv()
            for step in range(1, pd_size):
                across(owner, False, step, distance, piece).start()
    own.wait()
    for distance in order:
        for piece in range(pieces):
            direct(distance, piece).wait_send()
    for distance in [0] + order:
        for piece in range(pieces):
            owner = lax.rem(me - distance + ep_size, ep_size)
            for step in range(1, pd_size):
                copy = across(owner, distance == 0, step, distance, piece)
                copy.wait_send()
                copy.wait_recv()


def spread(source, block_shape, shared, pieces, collective_id, space):
    ep_size, pd_size = lax.axis_size("ep"), lax.axis_size("pd")
    return pl.pallas_call(
        functools.partial(spread_kernel, ep_size, pd_size, shared, pieces),
        out_shape=jax.ShapeDtypeStruct((pd_size, ep_size) + block_shape, source.dtype),
        in_specs=[pl.BlockSpec(memory_space=space)],
        out_specs=pl.BlockSpec(memory_space=space),
        scratch_shapes=[
            pltpu.SemaphoreType.DMA,
            pltpu.SemaphoreType.DMA((ep_size, pieces)),
            pltpu.SemaphoreType.DMA((ep_size, pieces)),
            pltpu.SemaphoreType.DMA((pd_size, ep_size, pieces)),
            pltpu.SemaphoreType.DMA((pd_size, ep_size, pieces)),
        ],
        compiler_params=pltpu.CompilerParams(
            collective_id=collective_id, has_side_effects=True, vmem_limit_bytes=40 * 2**20
        ),
    )(source)


def collect_kernel(
    ep_size,
    pd_size,
    partial_out,
    out,
    own_rows,
    other_rows,
    summed,
    own_sem,
    local_sem,
    pass_sem,
    got_sem,
    send_sem,
    recv_sem,
):
    me, column = lax.axis_index("ep"), lax.axis_index("pd")
    order = peer_order(ep_size) + [0]
    meet_peers(ep_size, pd_size)

    def across(distance, step):
        target = lax.rem(me + distance, ep_size)
        there = lax.rem(column + step, pd_size)
        return pltpu.make_async_remote_copy(
            src_ref=partial_out.at[there, target],
            dst_ref=other_rows.at[step - 1, target],
            send_sem=pass_sem.at[step, distance],
            recv_sem=got_sem.at[step, distance],
            device_id={"pd": there},
            device_id_type=pl.DeviceIdType.MESH,
        )

    def direct(distance):
        target = lax.rem(me + distance, ep_size)
        return pltpu.make_async_remote_copy(
            src_ref=summed.at[target],
            dst_ref=out.at[me],
            send_sem=send_sem.at[distance],
            recv_sem=recv_sem.at[distance],
            device_id={"ep": target},
            device_id_type=pl.DeviceIdType.MESH,
        )

    fetch = pltpu.make_async_copy(partial_out.at[column], own_rows, own_sem)
    fetch.start()
    for distance in order:
        for step in range(1, pd_size):
            across(distance, step).start()
    fetch.wait()
    for distance in order:
        target = lax.rem(me + distance, ep_size)
        total = own_rows[target].astype(jnp.float32)
        for step in range(1, pd_size):
            across(distance, step).wait_recv()
            total = total + other_rows[step - 1, target].astype(jnp.float32)
        summed[target] = total.astype(jnp.bfloat16)
        if distance:
            direct(distance).start()
    keep = pltpu.make_async_copy(summed.at[me], out.at[me], local_sem)
    keep.start()
    for distance in order:
        for step in range(1, pd_size):
            across(distance, step).wait_send()
        if distance:
            direct(distance).wait_send()
            direct(distance).wait_recv()
    keep.wait()


def collect(partial_out, collective_id):
    pd_size, ep_size, capacity, width = partial_out.shape
    return pl.pallas_call(
        functools.partial(collect_kernel, ep_size, pd_size),
        out_shape=jax.ShapeDtypeStruct((ep_size, capacity, width), jnp.bfloat16),
        in_specs=[pl.BlockSpec(memory_space=pl.ANY)],
        out_specs=pl.BlockSpec(memory_space=pl.ANY),
        scratch_shapes=[
            pltpu.VMEM((ep_size, capacity, width), jnp.bfloat16),
            pltpu.VMEM((pd_size - 1, ep_size, capacity, width), jnp.bfloat16),
            pltpu.VMEM((ep_size, capacity, width), jnp.bfloat16),
            pltpu.SemaphoreType.DMA,
            pltpu.SemaphoreType.DMA,
            pltpu.SemaphoreType.DMA((pd_size, ep_size)),
            pltpu.SemaphoreType.DMA((pd_size, ep_size)),
            pltpu.SemaphoreType.DMA((ep_size,)),
            pltpu.SemaphoreType.DMA((ep_size,)),
        ],
        compiler_params=pltpu.CompilerParams(
            collective_id=collective_id, has_side_effects=True, vmem_limit_bytes=48 * 2**20
        ),
    )(partial_out)


def per_device(
    hidden,
    moe_gain,
    expert_ids,
    gate_scores,
    gate_up,
    down_proj,
    kv_weight,
    attn_gain,
    kv_gain,
    prompt_lens,
    assign,
    latent_cache,
    cache_len,
    draft_hidden,
    queries,
):
    tok_rows, model_width = hidden.shape
    top_count = expert_ids.shape[1]
    experts = lax.axis_size("ep")
    quarters = lax.axis_size("pd")
    capacity = max(2, 2 * tok_rows * top_count // experts)
    normed = rms_norm(hidden.astype(jnp.float32), moe_gain).astype(jnp.bfloat16)
    route_weight = ROUTE_SCALE * gate_scores / jnp.sum(gate_scores, axis=-1, keepdims=True)
    flat_ids = expert_ids.reshape(-1)
    one_hot = (flat_ids[:, None] == jnp.arange(experts, dtype=jnp.int32)[None, :]).astype(jnp.int32)
    slot_rank = jnp.sum(
        one_hot * (jnp.cumsum(one_hot, axis=0, dtype=jnp.int32) - 1), axis=1, dtype=jnp.int32
    )
    target = flat_ids * capacity + slot_rank
    hits = jnp.arange(experts * capacity, dtype=jnp.int32)[:, None, None] == target.reshape(
        1, tok_rows, top_count
    )
    select = jnp.any(hits, axis=-1).astype(jnp.bfloat16)
    mix = jnp.sum(jnp.where(hits, route_weight[None], 0.0), axis=-1)
    outgoing = (
        jnp.dot(select, normed, preferred_element_type=jnp.float32)
        .astype(jnp.bfloat16)
        .reshape(experts, capacity, model_width)
    )
    gate_local = gate_up[0]
    down_local = down_proj[0]
    arrived = spread(outgoing, (capacity, model_width), False, 2, 1, pl.ANY)
    row_block = arrived.reshape(-1, model_width)
    gate_val = jnp.einsum("rd,dgf->rgf", row_block, gate_local, preferred_element_type=jnp.float32)
    partial_value = jnp.dot(
        (jax.nn.silu(gate_val[:, 0]) * gate_val[:, 1]).astype(jnp.bfloat16),
        down_local,
        preferred_element_type=jnp.float32,
    ).astype(jnp.bfloat16)
    partial_out = partial_value.reshape(arrived.shape)
    expert_out = collect(partial_out, 2).reshape(-1, model_width)
    mix_high = mix.astype(jnp.bfloat16)
    mix_low = (mix - mix_high.astype(jnp.float32)).astype(jnp.bfloat16)
    both = jnp.einsum(
        "asr,sd->ard",
        jnp.stack([mix_high, mix_low]),
        expert_out,
        preferred_element_type=jnp.float32,
    )
    mixture = both[0] + both[1]
    layer_out = (hidden.astype(jnp.float32) + mixture).astype(jnp.bfloat16)
    slot_count, step_count = (draft_hidden.shape[0], draft_hidden.shape[1])
    latent_width = kv_gain.shape[0]
    row_width = kv_weight.shape[1]
    kv_input = rms_norm(
        jnp.concatenate([layer_out, draft_hidden.reshape(-1, model_width)], axis=0).astype(
            jnp.float32
        ),
        attn_gain,
    ).astype(jnp.bfloat16)
    all_rows = kv_input.shape[0]
    slices = kv_input.reshape(all_rows, experts, -1).swapaxes(0, 1)
    gathered = lax.all_to_all(slices, "ep", split_axis=0, concat_axis=0, tiled=True)
    pieces = jnp.einsum(
        "erk,kl->erl", gathered, kv_weight, preferred_element_type=jnp.float32
    ).astype(jnp.bfloat16)
    compressed = jnp.sum(
        lax.all_to_all(pieces, "ep", split_axis=0, concat_axis=0, tiled=True),
        axis=0,
        dtype=jnp.float32,
    )
    latent_all = jnp.concatenate(
        [rms_norm(compressed[:, :latent_width], kv_gain), compressed[:, latent_width:]], axis=-1
    ).astype(jnp.bfloat16)
    prompt_latent = latent_all[:tok_rows]
    draft_latent = latent_all[tok_rows:].reshape(slot_count, step_count, row_width)
    device = lax.axis_index(("ep", "pd"))
    slot_ids = device * slot_count + jnp.arange(slot_count, dtype=jnp.int32)
    owner_hit = assign[None, :] == slot_ids[:, None]
    ends = jnp.cumsum(prompt_lens, dtype=jnp.int32)
    starts = ends - prompt_lens
    first_row = jnp.sum(jnp.where(owner_hit, starts[None, :], 0), axis=1, dtype=jnp.int32)
    block_len = jnp.sum(jnp.where(owner_hit, prompt_lens[None, :], 0), axis=1, dtype=jnp.int32)
    block_cap = 3 * tok_rows
    block_ids = jnp.arange(block_cap, dtype=jnp.int32)
    wanted = first_row[:, None] + block_ids[None, :]
    live_rows = block_ids[None, :] < block_len[:, None]
    shard_rows = spread(prompt_latent, prompt_latent.shape, True, 1, 3, pltpu.VMEM).reshape(
        -1, row_width
    )
    places = jnp.arange(quarters * experts * tok_rows, dtype=jnp.int32)
    from_pd, from_ep = places // (experts * tok_rows), places // tok_rows % experts
    row_index = (from_ep * quarters + from_pd) * tok_rows + places % tok_rows
    picker = ((row_index[None, None, :] == wanted[:, :, None]) & live_rows[:, :, None]).astype(
        jnp.bfloat16
    )
    blocks = jnp.einsum(
        "srn,nk->srk", picker, shard_rows, preferred_element_type=jnp.float32
    ).astype(jnp.bfloat16)
    decoded = jnp.stack(
        [
            slot_attention(
                queries[0],
                latent_cache[0],
                blocks[0],
                draft_latent[0],
                cache_len[0],
                block_len[0],
                latent_width,
            )
        ],
        axis=0,
    )
    return (layer_out, decoded)


def solution(mesh):
    in_specs = (
        P(("groups", "ep", "pd"), None),
        P(),
        P(("groups", "ep", "pd"), None),
        P(("groups", "ep", "pd"), None),
        P("ep", None, None, "pd"),
        P("ep", "pd", None),
        P("ep", None),
        P(),
        P(),
        P("groups"),
        P("groups"),
        P(("groups", "ep", "pd"), None, None),
        P(("groups", "ep", "pd")),
        P(("groups", "ep", "pd"), None, None),
        P(("groups", "ep", "pd"), None, None, None),
    )
    out_specs = (P(("groups", "ep", "pd"), None), P(("groups", "ep", "pd"), None, None, None))
    return jax.shard_map(
        per_device, mesh=mesh, in_specs=in_specs, out_specs=out_specs, check_vma=False
    )
```

```python
import functools

import jax
import jax.numpy as jnp
from jax import lax
from jax.experimental import pallas as pl
from jax.experimental.pallas import tpu as pltpu
from jax.sharding import PartitionSpec as P

NORM_EPSILON = 1e-06
ROUTE_SCALE = 2.5
SCORE_SCALE = 192.0 ** (-0.5)
ROPE_BASE = 10000.0


def rms_norm(values, gain):
    return (
        values * lax.rsqrt(jnp.mean(values * values, axis=-1, keepdims=True) + NORM_EPSILON) * gain
    )


def with_rope(row_vals, positions, rotary_width):
    latent_width = row_vals.shape[-1] - rotary_width
    rotary = row_vals[..., latent_width:].astype(jnp.float32)
    frequency = ROPE_BASE ** (
        -jnp.arange(rotary_width // 2, dtype=jnp.float32) * 2.0 / rotary_width
    )
    angles = positions.astype(jnp.float32)[..., None] * frequency
    even_part = rotary[..., 0::2]
    odd_part = rotary[..., 1::2]
    turned = jnp.stack(
        [
            even_part * jnp.cos(angles) - odd_part * jnp.sin(angles),
            even_part * jnp.sin(angles) + odd_part * jnp.cos(angles),
        ],
        axis=-1,
    ).reshape(rotary.shape)
    return jnp.concatenate([row_vals[..., :latent_width], turned.astype(jnp.bfloat16)], axis=-1)


def slot_attention(query, cache_rows, block_rows, draft_rows, cached, block_len, latent_width):
    step_count, head_count, row_width = query.shape
    rotary_width = row_width - latent_width
    block_cap = block_rows.shape[0]
    cache_cap = cache_rows.shape[0]
    block_pos = cached + jnp.arange(block_cap, dtype=jnp.int32)
    draft_pos = cached + block_len + jnp.arange(step_count, dtype=jnp.int32)
    key_rows = jnp.concatenate(
        [
            cache_rows,
            with_rope(block_rows, block_pos, rotary_width),
            with_rope(draft_rows, draft_pos, rotary_width),
        ],
        axis=0,
    )
    head_pos = jnp.broadcast_to(draft_pos[:, None], (step_count, head_count))
    turned_query = with_rope(query, head_pos, rotary_width).reshape(
        step_count * head_count, row_width
    )
    live_cache = jnp.broadcast_to(
        (jnp.arange(cache_cap, dtype=jnp.int32) < cached)[None, :], (step_count, cache_cap)
    )
    live_block = jnp.broadcast_to(
        (jnp.arange(block_cap, dtype=jnp.int32) < block_len)[None, :], (step_count, block_cap)
    )
    step_ids = jnp.arange(step_count, dtype=jnp.int32)
    live_draft = step_ids[None, :] <= step_ids[:, None]
    live_rows = jnp.concatenate([live_cache, live_block, live_draft], axis=1)
    scores = (
        jnp.einsum("qk,nk->qn", turned_query, key_rows, preferred_element_type=jnp.float32)
        * SCORE_SCALE
    )
    scores = scores.reshape(step_count, head_count, -1)
    scores = jnp.where(live_rows[:, None, :], scores, -1e30)
    peak = jnp.max(scores, axis=-1, keepdims=True)
    expo = jnp.exp(scores - peak)
    weights = (expo / jnp.sum(expo, axis=-1, keepdims=True)).astype(jnp.bfloat16)
    output = jnp.dot(
        weights.reshape(step_count * head_count, -1),
        key_rows[:, :latent_width],
        preferred_element_type=jnp.float32,
    )
    return output.reshape(step_count, head_count, latent_width).astype(jnp.bfloat16)


def near_and_far(count):
    return list(range(1, count // 2)), list(range(max(1, count // 2), count))


def interleave(far, near):
    merged = []
    for i in range(max(len(far), len(near))):
        merged += near[i : i + 1] + far[i : i + 1]
    return merged


def meet_peers(ep_size, pd_size):
    me, column = lax.axis_index("ep"), lax.axis_index("pd")
    barrier = pltpu.get_barrier_semaphore()
    for distance in range(1, ep_size):
        pl.semaphore_signal(
            barrier,
            inc=1,
            device_id={"ep": lax.rem(me + distance, ep_size)},
            device_id_type=pl.DeviceIdType.MESH,
        )
    for distance in range(1, pd_size):
        pl.semaphore_signal(
            barrier,
            inc=1,
            device_id={"pd": lax.rem(column + distance, pd_size)},
            device_id_type=pl.DeviceIdType.MESH,
        )
    pl.semaphore_wait(barrier, ep_size - 1 + pd_size - 1)


def remote(src, dst, send_sem, recv_sem, device):
    return pltpu.make_async_remote_copy(
        src_ref=src,
        dst_ref=dst,
        send_sem=send_sem,
        recv_sem=recv_sem,
        device_id=device,
        device_id_type=pl.DeviceIdType.MESH,
    )


def spread_kernel(
    ep_size, pd_size, pieces, window, src, out, local_sem, send_sem, recv_sem, pass_sem, got_sem
):
    me, column = lax.axis_index("ep"), lax.axis_index("pd")
    width = out.shape[-1] // pieces
    near, far = near_and_far(ep_size)
    near = [(mask, piece) for mask in near for piece in range(pieces)]
    far = [(mask, piece) for mask in far for piece in range(pieces)]
    meet_peers(ep_size, pd_size)

    def part(ref, piece):
        return ref if pieces == 1 else ref.at[:, pl.ds(piece * width, width)]

    def direct(mask, piece):
        return remote(
            part(src.at[me ^ mask], piece),
            part(out.at[column, me], piece),
            send_sem.at[mask, piece],
            recv_sem.at[mask, piece],
            {"ep": me ^ mask},
        )

    def across(mask, step, piece):
        return remote(
            part(src.at[me] if mask == 0 else out.at[column, me ^ mask], piece),
            part(out.at[column, me ^ mask], piece),
            pass_sem.at[step, mask, piece],
            got_sem.at[step, mask, piece],
            {"pd": lax.rem(column + step, pd_size)},
        )

    for item in far[:window]:
        direct(*item).start()
    for item in near:
        direct(*item).start()
    for piece in range(pieces):
        for step in range(1, pd_size):
            across(0, step, piece).start()
    own = pltpu.make_async_copy(src.at[me], out.at[column, me], local_sem)
    own.start()
    for item in interleave(far, near):
        mask, piece = item
        direct(*item).wait_recv()
        if item in far:
            later = far.index(item) + window
            direct(*item).wait_send()
            if later < len(far):
                direct(*far[later]).start()
        for step in range(1, pd_size):
            across(mask, step, piece).start()
    own.wait()
    for item in near:
        direct(*item).wait_send()
    for mask in range(ep_size):
        for piece in range(pieces):
            for step in range(1, pd_size):
                across(mask, step, piece).wait()


def spread(source, pieces, window, collective_id):
    ep_size, pd_size = lax.axis_size("ep"), lax.axis_size("pd")
    return pl.pallas_call(
        functools.partial(spread_kernel, ep_size, pd_size, pieces, window),
        out_shape=jax.ShapeDtypeStruct((pd_size,) + source.shape, source.dtype),
        in_specs=[pl.BlockSpec(memory_space=pl.ANY)],
        out_specs=pl.BlockSpec(memory_space=pl.ANY),
        scratch_shapes=[
            pltpu.SemaphoreType.DMA,
            pltpu.SemaphoreType.DMA((ep_size, pieces)),
            pltpu.SemaphoreType.DMA((ep_size, pieces)),
            pltpu.SemaphoreType.DMA((pd_size, ep_size, pieces)),
            pltpu.SemaphoreType.DMA((pd_size, ep_size, pieces)),
        ],
        compiler_params=pltpu.CompilerParams(
            collective_id=collective_id, has_side_effects=True, vmem_limit_bytes=40 * 2**20
        ),
    )(source)


def latent_kernel(
    ep_size,
    pd_size,
    token_rows,
    slices,
    weight,
    gain,
    out,
    own_latent,
    arrived,
    partial,
    returned,
    local_sem,
    slice_send,
    slice_recv,
    part_send,
    part_recv,
    send_sem,
    recv_sem,
    pass_sem,
    got_sem,
    side_send,
    side_recv,
):
    me, column = lax.axis_index("ep"), lax.axis_index("pd")
    near, far = near_and_far(ep_size)
    latent_width = gain.shape[-1]
    meet_peers(ep_size, pd_size)

    def outward(mask):
        return remote(
            slices.at[me ^ mask],
            arrived.at[me],
            slice_send.at[mask],
            slice_recv.at[mask],
            {"ep": me ^ mask},
        )

    def homeward(mask):
        return remote(
            partial.at[me ^ mask],
            returned.at[me],
            part_send.at[mask],
            part_recv.at[mask],
            {"ep": me ^ mask},
        )

    for mask in far + near:
        outward(mask).start()
    total = jnp.dot(slices[me], weight[...], preferred_element_type=jnp.float32)
    for mask in near + far:
        outward(mask).wait_recv()
        partial[me ^ mask] = jnp.dot(
            arrived[me ^ mask], weight[...], preferred_element_type=jnp.float32
        ).astype(jnp.bfloat16)
        homeward(mask).start()
    for mask in near + far:
        homeward(mask).wait_recv()
        total = total + returned[me ^ mask].astype(jnp.float32)
    lead = total[:, :latent_width]
    scale = lax.rsqrt(jnp.mean(lead * lead, axis=-1, keepdims=True) + NORM_EPSILON)
    own_latent[:, :latent_width] = (lead * scale * gain[...]).astype(jnp.bfloat16)
    own_latent[:, latent_width:] = total[:, latent_width:].astype(jnp.bfloat16)
    mine = own_latent.at[pl.ds(0, token_rows)]

    def direct(mask):
        return remote(
            mine,
            out.at[column, me],
            send_sem.at[mask],
            recv_sem.at[mask],
            {"ep": me ^ mask},
        )

    def across(mask, step):
        return remote(
            mine if mask == 0 else out.at[column, me ^ mask],
            out.at[column, me ^ mask],
            pass_sem.at[step, mask],
            got_sem.at[step, mask],
            {"pd": lax.rem(column + step, pd_size)},
        )

    def beside(mask, step):
        origin = lax.rem(column - step + pd_size, pd_size)
        here = out.at[origin, me ^ mask]
        return remote(
            mine if mask == 0 and step == 0 else here,
            here,
            side_send.at[step, mask],
            side_recv.at[step, mask],
            {"ep": me ^ 1},
        )

    chips = list(range(2, ep_size, 2))
    for step in range(1, pd_size):
        across(0, step).start()
    for mask in chips[::-1]:
        direct(mask).start()
    beside(0, 0).start()
    own = pltpu.make_async_copy(mine, out.at[column, me], local_sem)
    own.start()
    for mask in chips:
        direct(mask).wait_recv()
        for step in range(1, pd_size):
            across(mask, step).start()
        beside(mask, 0).start()
    for mask in [0] + chips:
        for step in range(1, pd_size):
            across(mask, step).wait_recv()
            beside(mask, step).start()
    own.wait()
    for mask in near + far:
        outward(mask).wait_send()
        homeward(mask).wait_send()
    for mask in chips:
        direct(mask).wait_send()
    for mask in [0] + chips:
        for step in range(pd_size):
            if step:
                across(mask, step).wait_send()
            beside(mask, step).wait()


def latents(slices, weight, gain, token_rows, collective_id):
    ep_size, pd_size = lax.axis_size("ep"), lax.axis_size("pd")
    rows, width = slices.shape[1], weight.shape[1]
    vmem = pl.BlockSpec(memory_space=pltpu.VMEM)
    dma = pltpu.SemaphoreType.DMA
    return pl.pallas_call(
        functools.partial(latent_kernel, ep_size, pd_size, token_rows),
        out_shape=(
            jax.ShapeDtypeStruct((pd_size, ep_size, token_rows, width), jnp.bfloat16),
            jax.ShapeDtypeStruct((rows, width), jnp.bfloat16),
        ),
        in_specs=[vmem] * 3,
        out_specs=(vmem, vmem),
        scratch_shapes=[
            pltpu.VMEM(slices.shape, jnp.bfloat16),
            pltpu.VMEM((ep_size, rows, width), jnp.bfloat16),
            pltpu.VMEM((ep_size, rows, width), jnp.bfloat16),
            dma,
            *([dma((ep_size,))] * 6),
            *([dma((pd_size, ep_size))] * 4),
        ],
        compiler_params=pltpu.CompilerParams(
            collective_id=collective_id, has_side_effects=True, vmem_limit_bytes=48 * 2**20
        ),
    )(slices, weight, gain)


def collect_kernel(
    ep_size,
    pd_size,
    pieces,
    window,
    partial_out,
    out,
    own_rows,
    other_rows,
    summed,
    own_sem,
    local_sem,
    pass_sem,
    got_sem,
    send_sem,
    recv_sem,
):
    me, column = lax.axis_index("ep"), lax.axis_index("pd")
    near, far = near_and_far(ep_size)
    width = out.shape[-1] // pieces
    items = [(mask, piece) for mask in far + near + [0] for piece in range(pieces)]
    meet_peers(ep_size, pd_size)

    def across(mask, piece, step):
        target = me ^ mask
        there = lax.rem(column + step, pd_size)
        columns = pl.ds(piece * width, width)
        return remote(
            partial_out.at[there, target, :, columns],
            other_rows.at[step - 1, target, :, columns],
            pass_sem.at[step, mask, piece],
            got_sem.at[step, mask, piece],
            {"pd": there},
        )

    def direct(mask, piece):
        columns = pl.ds(piece * width, width)
        return remote(
            summed.at[me ^ mask, :, columns],
            out.at[me, :, columns],
            send_sem.at[mask, piece],
            recv_sem.at[mask, piece],
            {"ep": me ^ mask},
        )

    for item in items[:window]:
        for step in range(1, pd_size):
            across(*item, step).start()
    fetch = pltpu.make_async_copy(partial_out.at[column], own_rows, own_sem)
    fetch.start()
    fetch.wait()
    for at, item in enumerate(items):
        mask, piece = item
        target = me ^ mask
        columns = pl.ds(piece * width, width)
        for step in range(1, pd_size):
            across(*item, step).wait()
            if at + window < len(items):
                across(*items[at + window], step).start()
        total = own_rows[target, :, columns].astype(jnp.float32)
        for step in range(1, pd_size):
            total = total + other_rows[step - 1, target, :, columns].astype(jnp.float32)
        summed[target, :, columns] = total.astype(jnp.bfloat16)
        if mask:
            direct(*item).start()
    keep = pltpu.make_async_copy(summed.at[me], out.at[me], local_sem)
    keep.start()
    for mask, piece in items:
        if mask:
            direct(mask, piece).wait()
    keep.wait()


def collect(partial_out, pieces, window, collective_id):
    pd_size, ep_size, capacity, width = partial_out.shape
    return pl.pallas_call(
        functools.partial(collect_kernel, ep_size, pd_size, pieces, window),
        out_shape=jax.ShapeDtypeStruct((ep_size, capacity, width), jnp.bfloat16),
        in_specs=[pl.BlockSpec(memory_space=pl.ANY)],
        out_specs=pl.BlockSpec(memory_space=pl.ANY),
        scratch_shapes=[
            pltpu.VMEM((ep_size, capacity, width), jnp.bfloat16),
            pltpu.VMEM((pd_size - 1, ep_size, capacity, width), jnp.bfloat16),
            pltpu.VMEM((ep_size, capacity, width), jnp.bfloat16),
            pltpu.SemaphoreType.DMA,
            pltpu.SemaphoreType.DMA,
            pltpu.SemaphoreType.DMA((pd_size, ep_size, pieces)),
            pltpu.SemaphoreType.DMA((pd_size, ep_size, pieces)),
            pltpu.SemaphoreType.DMA((ep_size, pieces)),
            pltpu.SemaphoreType.DMA((ep_size, pieces)),
        ],
        compiler_params=pltpu.CompilerParams(
            collective_id=collective_id, has_side_effects=True, vmem_limit_bytes=48 * 2**20
        ),
    )(partial_out)


def per_device(
    hidden,
    moe_gain,
    expert_ids,
    gate_scores,
    gate_up,
    down_proj,
    kv_weight,
    attn_gain,
    kv_gain,
    prompt_lens,
    assign,
    latent_cache,
    cache_len,
    draft_hidden,
    queries,
):
    tok_rows, model_width = hidden.shape
    top_count = expert_ids.shape[1]
    experts = lax.axis_size("ep")
    quarters = lax.axis_size("pd")
    capacity = max(2, 2 * tok_rows * top_count // experts)
    normed = rms_norm(hidden.astype(jnp.float32), moe_gain).astype(jnp.bfloat16)
    route_weight = ROUTE_SCALE * gate_scores / jnp.sum(gate_scores, axis=-1, keepdims=True)
    flat_ids = expert_ids.reshape(-1)
    one_hot = (flat_ids[:, None] == jnp.arange(experts, dtype=jnp.int32)[None, :]).astype(jnp.int32)
    slot_rank = jnp.sum(
        one_hot * (jnp.cumsum(one_hot, axis=0, dtype=jnp.int32) - 1), axis=1, dtype=jnp.int32
    )
    target = flat_ids * capacity + slot_rank
    hits = jnp.arange(experts * capacity, dtype=jnp.int32)[:, None, None] == target.reshape(
        1, tok_rows, top_count
    )
    select = jnp.any(hits, axis=-1).astype(jnp.bfloat16)
    mix = jnp.sum(jnp.where(hits, route_weight[None], 0.0), axis=-1)
    outgoing = (
        jnp.dot(select, normed, preferred_element_type=jnp.float32)
        .astype(jnp.bfloat16)
        .reshape(experts, capacity, model_width)
    )
    gate_local = gate_up[0]
    down_local = down_proj[0]
    arrived = spread(outgoing, 2, 2, 1)
    row_block = arrived.reshape(-1, model_width)
    gate_val = jnp.einsum("rd,dgf->rgf", row_block, gate_local, preferred_element_type=jnp.float32)
    partial_value = jnp.dot(
        (jax.nn.silu(gate_val[:, 0]) * gate_val[:, 1]).astype(jnp.bfloat16),
        down_local,
        preferred_element_type=jnp.float32,
    ).astype(jnp.bfloat16)
    partial_out = partial_value.reshape(arrived.shape)
    expert_out = collect(partial_out, 2, 2, 2).reshape(-1, model_width)
    mix_high = mix.astype(jnp.bfloat16)
    mix_low = (mix - mix_high.astype(jnp.float32)).astype(jnp.bfloat16)
    both = jnp.einsum(
        "asr,sd->ard",
        jnp.stack([mix_high, mix_low]),
        expert_out,
        preferred_element_type=jnp.float32,
    )
    mixture = both[0] + both[1]
    layer_out = (hidden.astype(jnp.float32) + mixture).astype(jnp.bfloat16)
    slot_count, step_count = (draft_hidden.shape[0], draft_hidden.shape[1])
    latent_width = kv_gain.shape[0]
    row_width = kv_weight.shape[1]
    kv_input = rms_norm(
        jnp.concatenate([layer_out, draft_hidden.reshape(-1, model_width)], axis=0).astype(
            jnp.float32
        ),
        attn_gain,
    ).astype(jnp.bfloat16)
    spare = -kv_input.shape[0] % 16
    slices = (
        jnp.pad(kv_input, ((0, spare), (0, 0))).reshape(-1, experts, kv_weight.shape[0])
    ).swapaxes(0, 1)
    shard_rows, own_latent = latents(slices, kv_weight, kv_gain[None], tok_rows, 3)
    draft_latent = own_latent[tok_rows : tok_rows + slot_count * step_count].reshape(
        slot_count, step_count, row_width
    )
    device = lax.axis_index(("ep", "pd"))
    slot_ids = device * slot_count + jnp.arange(slot_count, dtype=jnp.int32)
    owner_hit = assign[None, :] == slot_ids[:, None]
    ends = jnp.cumsum(prompt_lens, dtype=jnp.int32)
    starts = ends - prompt_lens
    first_row = jnp.sum(jnp.where(owner_hit, starts[None, :], 0), axis=1, dtype=jnp.int32)
    block_len = jnp.sum(jnp.where(owner_hit, prompt_lens[None, :], 0), axis=1, dtype=jnp.int32)
    block_cap = 3 * tok_rows
    block_ids = jnp.arange(block_cap, dtype=jnp.int32)
    wanted = first_row[:, None] + block_ids[None, :]
    live_rows = block_ids[None, :] < block_len[:, None]
    shard_rows = shard_rows.reshape(-1, row_width)
    places = jnp.arange(quarters * experts * tok_rows, dtype=jnp.int32)
    from_pd, from_ep = places // (experts * tok_rows), places // tok_rows % experts
    row_index = (from_ep * quarters + from_pd) * tok_rows + places % tok_rows
    picker = ((row_index[None, None, :] == wanted[:, :, None]) & live_rows[:, :, None]).astype(
        jnp.bfloat16
    )
    blocks = jnp.einsum(
        "srn,nk->srk", picker, shard_rows, preferred_element_type=jnp.float32
    ).astype(jnp.bfloat16)
    decoded = jnp.stack(
        [
            slot_attention(
                queries[0],
                latent_cache[0],
                blocks[0],
                draft_latent[0],
                cache_len[0],
                block_len[0],
                latent_width,
            )
        ],
        axis=0,
    )
    return (layer_out, decoded)


def solution(mesh):
    in_specs = (
        P(("groups", "ep", "pd"), None),
        P(),
        P(("groups", "ep", "pd"), None),
        P(("groups", "ep", "pd"), None),
        P("ep", None, None, "pd"),
        P("ep", "pd", None),
        P("ep", None),
        P(),
        P(),
        P("groups"),
        P("groups"),
        P(("groups", "ep", "pd"), None, None),
        P(("groups", "ep", "pd")),
        P(("groups", "ep", "pd"), None, None),
        P(("groups", "ep", "pd"), None, None, None),
    )
    out_specs = (P(("groups", "ep", "pd"), None), P(("groups", "ep", "pd"), None, None, None))
    return jax.shard_map(
        per_device, mesh=mesh, in_specs=in_specs, out_specs=out_specs, check_vma=False
    )
```

```python
import functools

import jax
import jax.numpy as jnp
from jax import lax
from jax.experimental import pallas as pl
from jax.experimental.pallas import tpu as pltpu
from jax.sharding import PartitionSpec as P

NORM_EPSILON = 1e-06
ROUTE_SCALE = 2.5
SCORE_SCALE = 192.0 ** (-0.5)
ROPE_BASE = 10000.0


def rms_norm(values, gain):
    return (
        values * lax.rsqrt(jnp.mean(values * values, axis=-1, keepdims=True) + NORM_EPSILON) * gain
    )


def with_rope(row_vals, positions, rotary_width):
    latent_width = row_vals.shape[-1] - rotary_width
    rotary = row_vals[..., latent_width:].astype(jnp.float32)
    lane = jnp.arange(rotary_width, dtype=jnp.int32)
    frequency = ROPE_BASE ** (-(lane // 2).astype(jnp.float32) * 2.0 / rotary_width)
    angles = positions.astype(jnp.float32)[..., None] * frequency
    pair = lane[:, None] == (lane ^ 1)[None, :]
    swap = jnp.where(pair, jnp.where(lane % 2 == 0, -1.0, 1.0)[None, :], 0.0).astype(jnp.bfloat16)
    partner = jnp.dot(
        row_vals[..., latent_width:], swap, preferred_element_type=jnp.float32
    )
    turned = rotary * jnp.cos(angles) + partner * jnp.sin(angles)
    return jnp.concatenate([row_vals[..., :latent_width], turned.astype(jnp.bfloat16)], axis=-1)


def slot_attention(query, cache_rows, block_rows, draft_rows, cached, block_len, latent_width):
    step_count, head_count, row_width = query.shape
    rotary_width = row_width - latent_width
    block_cap = block_rows.shape[0]
    cache_cap = cache_rows.shape[0]
    block_pos = cached + jnp.arange(block_cap, dtype=jnp.int32)
    draft_pos = cached + block_len + jnp.arange(step_count, dtype=jnp.int32)
    key_rows = jnp.concatenate(
        [
            cache_rows,
            with_rope(block_rows, block_pos, rotary_width),
            with_rope(draft_rows, draft_pos, rotary_width),
        ],
        axis=0,
    )
    turned_query = with_rope(query, draft_pos[:, None], rotary_width).reshape(
        step_count * head_count, row_width
    )
    live_cache = jnp.broadcast_to(
        (jnp.arange(cache_cap, dtype=jnp.int32) < cached)[None, :], (step_count, cache_cap)
    )
    live_block = jnp.broadcast_to(
        (jnp.arange(block_cap, dtype=jnp.int32) < block_len)[None, :], (step_count, block_cap)
    )
    step_ids = jnp.arange(step_count, dtype=jnp.int32)
    live_draft = step_ids[None, :] <= step_ids[:, None]
    live_rows = jnp.concatenate([live_cache, live_block, live_draft], axis=1)
    scores = (
        jnp.einsum("qk,nk->qn", turned_query, key_rows, preferred_element_type=jnp.float32)
        * SCORE_SCALE
    )
    scores = scores.reshape(step_count, head_count, -1)
    scores = jnp.where(live_rows[:, None, :], scores, -1e30)
    peak = jnp.max(scores, axis=-1, keepdims=True)
    expo = jnp.exp(scores - peak)
    weights = (expo / jnp.sum(expo, axis=-1, keepdims=True)).astype(jnp.bfloat16)
    output = jnp.dot(
        weights.reshape(step_count * head_count, -1),
        key_rows[:, :latent_width],
        preferred_element_type=jnp.float32,
    )
    return output.reshape(step_count, head_count, latent_width).astype(jnp.bfloat16)


def near_and_far(count):
    return list(range(1, count // 2)), list(range(max(1, count // 2), count))


def interleave(far, near):
    merged = []
    for i in range(max(len(far), len(near))):
        merged += near[i : i + 1] + far[i : i + 1]
    return merged


def meet_peers(ep_size, pd_size):
    me, column = lax.axis_index("ep"), lax.axis_index("pd")
    barrier = pltpu.get_barrier_semaphore()
    for distance in range(1, ep_size):
        pl.semaphore_signal(
            barrier,
            inc=1,
            device_id={"ep": lax.rem(me + distance, ep_size)},
            device_id_type=pl.DeviceIdType.MESH,
        )
    for distance in range(1, pd_size):
        pl.semaphore_signal(
            barrier,
            inc=1,
            device_id={"pd": lax.rem(column + distance, pd_size)},
            device_id_type=pl.DeviceIdType.MESH,
        )
    pl.semaphore_wait(barrier, ep_size - 1 + pd_size - 1)


def remote(src, dst, send_sem, recv_sem, device):
    return pltpu.make_async_remote_copy(
        src_ref=src,
        dst_ref=dst,
        send_sem=send_sem,
        recv_sem=recv_sem,
        device_id=device,
        device_id_type=pl.DeviceIdType.MESH,
    )


def spread_kernel(
    ep_size,
    pd_size,
    pieces,
    window,
    src,
    weight,
    out,
    weight_pair,
    local_sem,
    weight_sem,
    pair_send,
    pair_recv,
    send_sem,
    recv_sem,
    pass_sem,
    got_sem,
):
    me, column = lax.axis_index("ep"), lax.axis_index("pd")
    width = out.shape[-1] // pieces
    near, far = near_and_far(ep_size)
    near = [(mask, piece) for mask in near for piece in range(pieces)]
    far = [(mask, piece) for mask in far for piece in range(pieces)]
    meet_peers(ep_size, pd_size)

    def part(ref, piece):
        return ref if pieces == 1 else ref.at[:, pl.ds(piece * width, width)]

    def direct(mask, piece):
        return remote(
            part(src.at[me ^ mask], piece),
            part(out.at[column, me], piece),
            send_sem.at[mask, piece],
            recv_sem.at[mask, piece],
            {"ep": me ^ mask},
        )

    def across(mask, step, piece):
        return remote(
            part(src.at[me] if mask == 0 else out.at[column, me ^ mask], piece),
            part(out.at[column, me ^ mask], piece),
            pass_sem.at[step, mask, piece],
            got_sem.at[step, mask, piece],
            {"pd": lax.rem(column + step, pd_size)},
        )

    for item in far[:window]:
        direct(*item).start()
    for item in near:
        direct(*item).start()
    for piece in range(pieces):
        for step in range(1, pd_size):
            across(0, step, piece).start()
    own = pltpu.make_async_copy(src.at[me], out.at[column, me], local_sem)
    own.start()
    core = lax.rem(me, 2)
    keep = pltpu.make_async_copy(weight, weight_pair.at[core], weight_sem)
    keep.start()
    give = remote(weight, weight_pair.at[core], pair_send, pair_recv, {"ep": me ^ 1})
    give.start()
    for item in interleave(far, near):
        mask, piece = item
        direct(*item).wait_recv()
        if item in far:
            later = far.index(item) + window
            direct(*item).wait_send()
            if later < len(far):
                direct(*far[later]).start()
        for step in range(1, pd_size):
            across(mask, step, piece).start()
    own.wait()
    keep.wait()
    give.wait()
    for item in near:
        direct(*item).wait_send()
    for mask in range(ep_size):
        for piece in range(pieces):
            for step in range(1, pd_size):
                across(mask, step, piece).wait()


def spread(source, weight, pieces, window, collective_id):
    ep_size, pd_size = lax.axis_size("ep"), lax.axis_size("pd")
    return pl.pallas_call(
        functools.partial(spread_kernel, ep_size, pd_size, pieces, window),
        out_shape=(
            jax.ShapeDtypeStruct((pd_size,) + source.shape, source.dtype),
            jax.ShapeDtypeStruct((2,) + weight.shape, weight.dtype),
        ),
        in_specs=[pl.BlockSpec(memory_space=pl.ANY)] * 2,
        out_specs=(pl.BlockSpec(memory_space=pl.ANY),) * 2,
        scratch_shapes=[
            *([pltpu.SemaphoreType.DMA] * 4),
            pltpu.SemaphoreType.DMA((ep_size, pieces)),
            pltpu.SemaphoreType.DMA((ep_size, pieces)),
            pltpu.SemaphoreType.DMA((pd_size, ep_size, pieces)),
            pltpu.SemaphoreType.DMA((pd_size, ep_size, pieces)),
        ],
        compiler_params=pltpu.CompilerParams(
            collective_id=collective_id, has_side_effects=True, vmem_limit_bytes=40 * 2**20
        ),
    )(source, weight)


def latent_kernel(
    ep_size,
    pd_size,
    token_rows,
    slices,
    weight,
    gain,
    out,
    own_latent,
    arrived,
    partial,
    returned,
    local_sem,
    slice_send,
    slice_recv,
    part_send,
    part_recv,
    send_sem,
    recv_sem,
    pass_sem,
    got_sem,
    side_send,
    side_recv,
):
    me, column = lax.axis_index("ep"), lax.axis_index("pd")
    here = lax.div(me, 2)
    chips = list(range(2, ep_size, 2))
    near = [mask for mask in chips if 2 * mask < ep_size]
    far = [mask for mask in chips if 2 * mask >= ep_size]
    latent_width = gain.shape[-1]
    meet_peers(ep_size, pd_size)

    def chip(mask):
        return lax.div(me ^ mask, 2)

    def outward(mask):
        return remote(
            slices.at[chip(mask)],
            arrived.at[here],
            slice_send.at[mask],
            slice_recv.at[mask],
            {"ep": me ^ mask},
        )

    def homeward(mask):
        return remote(
            partial.at[chip(mask)],
            returned.at[here],
            part_send.at[mask],
            part_recv.at[mask],
            {"ep": me ^ mask},
        )

    for mask in far[:1] + near:
        outward(mask).start()
    total = jnp.dot(slices[here], weight[...], preferred_element_type=jnp.float32)
    for at, mask in enumerate(far):
        outward(mask).wait_send()
        for later in far[at + 1 : at + 2]:
            outward(later).start()
        for ready in [mask] if at else near + [mask]:
            outward(ready).wait_recv()
            partial[chip(ready)] = jnp.dot(
                arrived[chip(ready)], weight[...], preferred_element_type=jnp.float32
            ).astype(jnp.bfloat16)
            homeward(ready).start()
    for mask in chips:
        homeward(mask).wait_recv()
        total = total + returned[chip(mask)].astype(jnp.float32)
    lead = total[:, :latent_width]
    scale = lax.rsqrt(jnp.mean(lead * lead, axis=-1, keepdims=True) + NORM_EPSILON)
    own_latent[:, :latent_width] = (lead * scale * gain[...]).astype(jnp.bfloat16)
    own_latent[:, latent_width:] = total[:, latent_width:].astype(jnp.bfloat16)
    mine = own_latent.at[pl.ds(0, token_rows)]

    def direct(mask):
        return remote(
            mine,
            out.at[column, me],
            send_sem.at[mask],
            recv_sem.at[mask],
            {"ep": me ^ mask},
        )

    def across(mask, step):
        return remote(
            mine if mask == 0 else out.at[column, me ^ mask],
            out.at[column, me ^ mask],
            pass_sem.at[step, mask],
            got_sem.at[step, mask],
            {"pd": lax.rem(column + step, pd_size)},
        )

    def beside(mask, step):
        origin = lax.rem(column - step + pd_size, pd_size)
        here = out.at[origin, me ^ mask]
        return remote(
            mine if mask == 0 and step == 0 else here,
            here,
            side_send.at[step, mask],
            side_recv.at[step, mask],
            {"ep": me ^ 1},
        )

    for step in range(1, pd_size):
        across(0, step).start()
    for mask in chips[::-1]:
        direct(mask).start()
    beside(0, 0).start()
    own = pltpu.make_async_copy(mine, out.at[column, me], local_sem)
    own.start()
    for mask in chips:
        direct(mask).wait_recv()
        for step in range(1, pd_size):
            across(mask, step).start()
        beside(mask, 0).start()
    for mask in [0] + chips:
        for step in range(1, pd_size):
            across(mask, step).wait_recv()
            beside(mask, step).start()
    own.wait()
    for mask in near:
        outward(mask).wait_send()
    for mask in chips:
        homeward(mask).wait_send()
        direct(mask).wait_send()
    for mask in [0] + chips:
        for step in range(pd_size):
            if step:
                across(mask, step).wait_send()
            beside(mask, step).wait()


def latents(slices, weight, gain, token_rows, collective_id):
    ep_size, pd_size = lax.axis_size("ep"), lax.axis_size("pd")
    rows, width = slices.shape[1], weight.shape[1]
    vmem = pl.BlockSpec(memory_space=pltpu.VMEM)
    dma = pltpu.SemaphoreType.DMA
    return pl.pallas_call(
        functools.partial(latent_kernel, ep_size, pd_size, token_rows),
        out_shape=(
            jax.ShapeDtypeStruct((pd_size, ep_size, token_rows, width), jnp.bfloat16),
            jax.ShapeDtypeStruct((rows, width), jnp.bfloat16),
        ),
        in_specs=[vmem] * 3,
        out_specs=(vmem, vmem),
        scratch_shapes=[
            pltpu.VMEM(slices.shape, jnp.bfloat16),
            pltpu.VMEM((ep_size // 2, rows, width), jnp.bfloat16),
            pltpu.VMEM((ep_size // 2, rows, width), jnp.bfloat16),
            dma,
            *([dma((ep_size,))] * 6),
            *([dma((pd_size, ep_size))] * 4),
        ],
        compiler_params=pltpu.CompilerParams(
            collective_id=collective_id, has_side_effects=True, vmem_limit_bytes=48 * 2**20
        ),
    )(slices, weight, gain)


def collect_kernel(
    ep_size,
    pd_size,
    pieces,
    window,
    partial_out,
    out,
    own_rows,
    other_rows,
    summed,
    own_sem,
    local_sem,
    pass_sem,
    got_sem,
    send_sem,
    recv_sem,
):
    me, column = lax.axis_index("ep"), lax.axis_index("pd")
    near, far = near_and_far(ep_size)
    width = out.shape[-1] // pieces
    items = [(mask, piece) for mask in far + near + [0] for piece in range(pieces)]
    meet_peers(ep_size, pd_size)

    def across(mask, piece, step):
        target = me ^ mask
        there = lax.rem(column + step, pd_size)
        columns = pl.ds(piece * width, width)
        return remote(
            partial_out.at[there, target, :, columns],
            other_rows.at[step - 1, target, :, columns],
            pass_sem.at[step, mask, piece],
            got_sem.at[step, mask, piece],
            {"pd": there},
        )

    def direct(mask, piece):
        columns = pl.ds(piece * width, width)
        return remote(
            summed.at[me ^ mask, :, columns],
            out.at[me, :, columns],
            send_sem.at[mask, piece],
            recv_sem.at[mask, piece],
            {"ep": me ^ mask},
        )

    for item in items[:window]:
        for step in range(1, pd_size):
            across(*item, step).start()
    fetch = pltpu.make_async_copy(partial_out.at[column], own_rows, own_sem)
    fetch.start()
    fetch.wait()
    for at, item in enumerate(items):
        mask, piece = item
        target = me ^ mask
        columns = pl.ds(piece * width, width)
        for step in range(1, pd_size):
            across(*item, step).wait()
            if at + window < len(items):
                across(*items[at + window], step).start()
        total = own_rows[target, :, columns].astype(jnp.float32)
        for step in range(1, pd_size):
            total = total + other_rows[step - 1, target, :, columns].astype(jnp.float32)
        summed[target, :, columns] = total.astype(jnp.bfloat16)
        if mask:
            direct(*item).start()
    keep = pltpu.make_async_copy(summed.at[me], out.at[me], local_sem)
    keep.start()
    for mask, piece in items:
        if mask:
            direct(mask, piece).wait()
    keep.wait()


def collect(partial_out, pieces, window, collective_id):
    pd_size, ep_size, capacity, width = partial_out.shape
    return pl.pallas_call(
        functools.partial(collect_kernel, ep_size, pd_size, pieces, window),
        out_shape=jax.ShapeDtypeStruct((ep_size, capacity, width), jnp.bfloat16),
        in_specs=[pl.BlockSpec(memory_space=pl.ANY)],
        out_specs=pl.BlockSpec(memory_space=pl.ANY),
        scratch_shapes=[
            pltpu.VMEM((ep_size, capacity, width), jnp.bfloat16),
            pltpu.VMEM((pd_size - 1, ep_size, capacity, width), jnp.bfloat16),
            pltpu.VMEM((ep_size, capacity, width), jnp.bfloat16),
            pltpu.SemaphoreType.DMA,
            pltpu.SemaphoreType.DMA,
            pltpu.SemaphoreType.DMA((pd_size, ep_size, pieces)),
            pltpu.SemaphoreType.DMA((pd_size, ep_size, pieces)),
            pltpu.SemaphoreType.DMA((ep_size, pieces)),
            pltpu.SemaphoreType.DMA((ep_size, pieces)),
        ],
        compiler_params=pltpu.CompilerParams(
            collective_id=collective_id, has_side_effects=True, vmem_limit_bytes=48 * 2**20
        ),
    )(partial_out)


def per_device(
    hidden,
    moe_gain,
    expert_ids,
    gate_scores,
    gate_up,
    down_proj,
    kv_weight,
    attn_gain,
    kv_gain,
    prompt_lens,
    assign,
    latent_cache,
    cache_len,
    draft_hidden,
    queries,
):
    tok_rows, model_width = hidden.shape
    top_count = expert_ids.shape[1]
    experts = lax.axis_size("ep")
    quarters = lax.axis_size("pd")
    capacity = max(2, 2 * tok_rows * top_count // experts)
    normed = rms_norm(hidden.astype(jnp.float32), moe_gain).astype(jnp.bfloat16)
    route_weight = ROUTE_SCALE * gate_scores / jnp.sum(gate_scores, axis=-1, keepdims=True)
    flat_ids = expert_ids.reshape(-1)
    one_hot = (flat_ids[:, None] == jnp.arange(experts, dtype=jnp.int32)[None, :]).astype(jnp.int32)
    slot_rank = jnp.sum(
        one_hot * (jnp.cumsum(one_hot, axis=0, dtype=jnp.int32) - 1), axis=1, dtype=jnp.int32
    )
    target = flat_ids * capacity + slot_rank
    hits = jnp.arange(experts * capacity, dtype=jnp.int32)[:, None, None] == target.reshape(
        1, tok_rows, top_count
    )
    select = jnp.any(hits, axis=-1).astype(jnp.bfloat16)
    mix = jnp.sum(jnp.where(hits, route_weight[None], 0.0), axis=-1)
    outgoing = (
        jnp.dot(select, normed, preferred_element_type=jnp.float32)
        .astype(jnp.bfloat16)
        .reshape(experts, capacity, model_width)
    )
    gate_local = gate_up[0]
    down_local = down_proj[0]
    arrived, weight_pair = spread(outgoing, kv_weight, 4, 4, 1)
    row_block = arrived.reshape(-1, model_width)
    gate_val = jnp.einsum("rd,dgf->rgf", row_block, gate_local, preferred_element_type=jnp.float32)
    partial_value = jnp.dot(
        (jax.nn.silu(gate_val[:, 0]) * gate_val[:, 1]).astype(jnp.bfloat16),
        down_local,
        preferred_element_type=jnp.float32,
    ).astype(jnp.bfloat16)
    partial_out = partial_value.reshape(arrived.shape)
    expert_out = collect(partial_out, 4, 6, 2).reshape(-1, model_width)
    mix_high = mix.astype(jnp.bfloat16)
    mix_low = (mix - mix_high.astype(jnp.float32)).astype(jnp.bfloat16)
    both = jnp.einsum(
        "asr,sd->ard",
        jnp.stack([mix_high, mix_low]),
        expert_out,
        preferred_element_type=jnp.float32,
    )
    mixture = both[0] + both[1]
    layer_out = (hidden.astype(jnp.float32) + mixture).astype(jnp.bfloat16)
    slot_count, step_count = (draft_hidden.shape[0], draft_hidden.shape[1])
    latent_width = kv_gain.shape[0]
    row_width = kv_weight.shape[1]
    kv_input = rms_norm(
        jnp.concatenate([layer_out, draft_hidden.reshape(-1, model_width)], axis=0).astype(
            jnp.float32
        ),
        attn_gain,
    ).astype(jnp.bfloat16)
    spare = -kv_input.shape[0] % 16
    slices = (
        jnp.pad(kv_input, ((0, spare), (0, 0))).reshape(-1, experts // 2, 2 * kv_weight.shape[0])
    ).swapaxes(0, 1)
    shard_rows, own_latent = latents(
        slices, weight_pair.reshape(-1, row_width), kv_gain[None], tok_rows, 3
    )
    draft_latent = own_latent[tok_rows : tok_rows + slot_count * step_count].reshape(
        slot_count, step_count, row_width
    )
    device = lax.axis_index(("ep", "pd"))
    slot_ids = device * slot_count + jnp.arange(slot_count, dtype=jnp.int32)
    owner_hit = assign[None, :] == slot_ids[:, None]
    ends = jnp.cumsum(prompt_lens, dtype=jnp.int32)
    starts = ends - prompt_lens
    first_row = jnp.sum(jnp.where(owner_hit, starts[None, :], 0), axis=1, dtype=jnp.int32)
    block_len = jnp.sum(jnp.where(owner_hit, prompt_lens[None, :], 0), axis=1, dtype=jnp.int32)
    block_cap = 3 * tok_rows
    block_ids = jnp.arange(block_cap, dtype=jnp.int32)
    wanted = first_row[:, None] + block_ids[None, :]
    live_rows = block_ids[None, :] < block_len[:, None]
    shard_rows = shard_rows.reshape(-1, row_width)
    places = jnp.arange(quarters * experts * tok_rows, dtype=jnp.int32)
    from_pd, from_ep = places // (experts * tok_rows), places // tok_rows % experts
    row_index = (from_ep * quarters + from_pd) * tok_rows + places % tok_rows
    picker = ((row_index[None, None, :] == wanted[:, :, None]) & live_rows[:, :, None]).astype(
        jnp.bfloat16
    )
    blocks = jnp.einsum(
        "srn,nk->srk", picker, shard_rows, preferred_element_type=jnp.float32
    ).astype(jnp.bfloat16)
    decoded = jnp.stack(
        [
            slot_attention(
                queries[0],
                latent_cache[0],
                blocks[0],
                draft_latent[0],
                cache_len[0],
                block_len[0],
                latent_width,
            )
        ],
        axis=0,
    )
    return (layer_out, decoded)


def solution(mesh):
    in_specs = (
        P(("groups", "ep", "pd"), None),
        P(),
        P(("groups", "ep", "pd"), None),
        P(("groups", "ep", "pd"), None),
        P("ep", None, None, "pd"),
        P("ep", "pd", None),
        P("ep", None),
        P(),
        P(),
        P("groups"),
        P("groups"),
        P(("groups", "ep", "pd"), None, None),
        P(("groups", "ep", "pd")),
        P(("groups", "ep", "pd"), None, None),
        P(("groups", "ep", "pd"), None, None, None),
    )
    out_specs = (P(("groups", "ep", "pd"), None), P(("groups", "ep", "pd"), None, None, None))
    return jax.shard_map(
        per_device, mesh=mesh, in_specs=in_specs, out_specs=out_specs, check_vma=False
    )
```

```python
import functools

import jax
import jax.numpy as jnp
from jax import lax
from jax.experimental import pallas as pl
from jax.experimental.pallas import tpu as pltpu
from jax.sharding import PartitionSpec as P

NORM_EPSILON = 1e-06
ROUTE_SCALE = 2.5
SCORE_SCALE = 192.0 ** (-0.5)
ROPE_BASE = 10000.0


def rms_norm(values, gain):
    return (
        values * lax.rsqrt(jnp.mean(values * values, axis=-1, keepdims=True) + NORM_EPSILON) * gain
    )


def with_rope(row_vals, positions, rotary_width):
    latent_width = row_vals.shape[-1] - rotary_width
    rotary = row_vals[..., latent_width:].astype(jnp.float32)
    lane = jnp.arange(rotary_width, dtype=jnp.int32)
    frequency = ROPE_BASE ** (-(lane // 2).astype(jnp.float32) * 2.0 / rotary_width)
    angles = positions.astype(jnp.float32)[..., None] * frequency
    pair = lane[:, None] == (lane ^ 1)[None, :]
    swap = jnp.where(pair, jnp.where(lane % 2 == 0, -1.0, 1.0)[None, :], 0.0).astype(jnp.bfloat16)
    partner = jnp.dot(
        row_vals[..., latent_width:], swap, preferred_element_type=jnp.float32
    )
    turned = rotary * jnp.cos(angles) + partner * jnp.sin(angles)
    return jnp.concatenate([row_vals[..., :latent_width], turned.astype(jnp.bfloat16)], axis=-1)


def slot_attention(query, cache_rows, block_rows, draft_rows, cached, block_len, latent_width):
    step_count, head_count, row_width = query.shape
    rotary_width = row_width - latent_width
    block_cap = block_rows.shape[0]
    cache_cap = cache_rows.shape[0]
    block_pos = cached + jnp.arange(block_cap, dtype=jnp.int32)
    draft_pos = cached + block_len + jnp.arange(step_count, dtype=jnp.int32)
    key_rows = jnp.concatenate(
        [
            cache_rows,
            with_rope(block_rows, block_pos, rotary_width),
            with_rope(draft_rows, draft_pos, rotary_width),
        ],
        axis=0,
    )
    turned_query = with_rope(query, draft_pos[:, None], rotary_width).reshape(
        step_count * head_count, row_width
    )
    live_cache = jnp.broadcast_to(
        (jnp.arange(cache_cap, dtype=jnp.int32) < cached)[None, :], (step_count, cache_cap)
    )
    live_block = jnp.broadcast_to(
        (jnp.arange(block_cap, dtype=jnp.int32) < block_len)[None, :], (step_count, block_cap)
    )
    step_ids = jnp.arange(step_count, dtype=jnp.int32)
    live_draft = step_ids[None, :] <= step_ids[:, None]
    live_rows = jnp.concatenate([live_cache, live_block, live_draft], axis=1)
    scores = (
        jnp.einsum("qk,nk->qn", turned_query, key_rows, preferred_element_type=jnp.float32)
        * SCORE_SCALE
    )
    scores = scores.reshape(step_count, head_count, -1)
    scores = jnp.where(live_rows[:, None, :], scores, -1e30)
    peak = jnp.max(scores, axis=-1, keepdims=True)
    expo = jnp.exp(scores - peak)
    weights = (expo / jnp.sum(expo, axis=-1, keepdims=True)).astype(jnp.bfloat16)
    output = jnp.dot(
        weights.reshape(step_count * head_count, -1),
        key_rows[:, :latent_width],
        preferred_element_type=jnp.float32,
    )
    return output.reshape(step_count, head_count, latent_width).astype(jnp.bfloat16)


def near_and_far(count):
    return list(range(1, count // 2)), list(range(max(1, count // 2), count))


def interleave(far, near):
    merged = []
    for i in range(max(len(far), len(near))):
        merged += near[i : i + 1] + far[i : i + 1]
    return merged


def meet_peers(ep_size, pd_size):
    me, column = lax.axis_index("ep"), lax.axis_index("pd")
    barrier = pltpu.get_barrier_semaphore()
    for distance in range(1, ep_size):
        pl.semaphore_signal(
            barrier,
            inc=1,
            device_id={"ep": lax.rem(me + distance, ep_size)},
            device_id_type=pl.DeviceIdType.MESH,
        )
    for distance in range(1, pd_size):
        pl.semaphore_signal(
            barrier,
            inc=1,
            device_id={"pd": lax.rem(column + distance, pd_size)},
            device_id_type=pl.DeviceIdType.MESH,
        )
    pl.semaphore_wait(barrier, ep_size - 1 + pd_size - 1)


def remote(src, dst, send_sem, recv_sem, device):
    return pltpu.make_async_remote_copy(
        src_ref=src,
        dst_ref=dst,
        send_sem=send_sem,
        recv_sem=recv_sem,
        device_id=device,
        device_id_type=pl.DeviceIdType.MESH,
    )


def spread_kernel(
    ep_size,
    pd_size,
    pieces,
    window,
    select,
    rows,
    weight,
    drafts,
    out,
    weight_pair,
    draft_slices,
    src,
    draft_own,
    draft_send,
    draft_recv,
    local_sem,
    weight_sem,
    pair_send,
    pair_recv,
    send_sem,
    recv_sem,
    pass_sem,
    got_sem,
):
    me, column = lax.axis_index("ep"), lax.axis_index("pd")
    width = out.shape[-1] // pieces
    near, far = near_and_far(ep_size)
    near = [(mask, piece) for mask in near for piece in range(pieces)]
    far = [(mask, piece) for mask in far for piece in range(pieces)]
    meet_peers(ep_size, pd_size)

    def part(ref, piece):
        return ref if pieces == 1 else ref.at[:, pl.ds(piece * width, width)]

    def direct(mask, piece):
        return remote(
            part(src.at[me ^ mask], piece),
            part(out.at[column, me], piece),
            send_sem.at[mask, piece],
            recv_sem.at[mask, piece],
            {"ep": me ^ mask},
        )

    def across(mask, step, piece):
        return remote(
            part(src.at[me] if mask == 0 else out.at[column, me ^ mask], piece),
            part(out.at[column, me ^ mask], piece),
            pass_sem.at[step, mask, piece],
            got_sem.at[step, mask, piece],
            {"pd": lax.rem(column + step, pd_size)},
        )

    def draft(mask):
        return remote(
            drafts.at[lax.div(me ^ mask, 2)],
            draft_slices.at[lax.div(me, 2)],
            draft_send.at[mask],
            draft_recv.at[mask],
            {"ep": me ^ mask},
        )

    def fill(mask):
        src[me ^ mask] = jnp.dot(
            select[me ^ mask], rows[...], preferred_element_type=jnp.float32
        ).astype(jnp.bfloat16)

    first = list(dict.fromkeys(mask for mask, _ in far[:window]))
    for mask in first:
        fill(mask)
    for item in far[:window]:
        direct(*item).start()
    fill(0)
    for piece in range(pieces):
        for step in range(1, pd_size):
            across(0, step, piece).start()
    for item in near:
        if item[1] == 0:
            fill(item[0])
        direct(*item).start()
    for mask in list(dict.fromkeys(mask for mask, _ in far)):
        if mask not in first:
            fill(mask)
    stay = pltpu.make_async_copy(
        drafts.at[lax.div(me, 2)], draft_slices.at[lax.div(me, 2)], draft_own
    )
    stay.start()
    for mask in range(2, ep_size, 2):
        draft(mask).start()
    own = pltpu.make_async_copy(src.at[me], out.at[column, me], local_sem)
    own.start()
    core = lax.rem(me, 2)
    keep = pltpu.make_async_copy(weight, weight_pair.at[core], weight_sem)
    keep.start()
    give = remote(weight, weight_pair.at[core], pair_send, pair_recv, {"ep": me ^ 1})
    give.start()
    for item in interleave(far, near):
        mask, piece = item
        direct(*item).wait_recv()
        if item in far:
            later = far.index(item) + window
            direct(*item).wait_send()
            if later < len(far):
                direct(*far[later]).start()
        for step in range(1, pd_size):
            across(mask, step, piece).start()
    own.wait()
    keep.wait()
    give.wait()
    stay.wait()
    for mask in range(2, ep_size, 2):
        draft(mask).wait()
    for item in near:
        direct(*item).wait_send()
    for mask in range(ep_size):
        for piece in range(pieces):
            for step in range(1, pd_size):
                across(mask, step, piece).wait()


def spread(select, rows, weight, drafts, pieces, window, collective_id):
    ep_size, pd_size = lax.axis_size("ep"), lax.axis_size("pd")
    block_shape = select.shape[:2] + rows.shape[1:]
    return pl.pallas_call(
        functools.partial(spread_kernel, ep_size, pd_size, pieces, window),
        out_shape=(
            jax.ShapeDtypeStruct((pd_size,) + block_shape, rows.dtype),
            jax.ShapeDtypeStruct((2,) + weight.shape, weight.dtype),
            jax.ShapeDtypeStruct(drafts.shape, drafts.dtype),
        ),
        in_specs=[pl.BlockSpec(memory_space=pltpu.VMEM)] * 2
        + [pl.BlockSpec(memory_space=pl.ANY)] * 2,
        out_specs=(pl.BlockSpec(memory_space=pl.ANY),) * 3,
        scratch_shapes=[
            pltpu.VMEM(block_shape, rows.dtype),
            pltpu.SemaphoreType.DMA,
            pltpu.SemaphoreType.DMA((ep_size,)),
            pltpu.SemaphoreType.DMA((ep_size,)),
            *([pltpu.SemaphoreType.DMA] * 4),
            pltpu.SemaphoreType.DMA((ep_size, pieces)),
            pltpu.SemaphoreType.DMA((ep_size, pieces)),
            pltpu.SemaphoreType.DMA((pd_size, ep_size, pieces)),
            pltpu.SemaphoreType.DMA((pd_size, ep_size, pieces)),
        ],
        compiler_params=pltpu.CompilerParams(
            collective_id=collective_id, has_side_effects=True, vmem_limit_bytes=40 * 2**20
        ),
    )(select, rows, weight, drafts)


def latent_kernel(
    ep_size,
    pd_size,
    token_rows,
    slices,
    draft_slices,
    weight,
    gain,
    out,
    own_latent,
    arrived,
    partial,
    returned,
    local_sem,
    slice_send,
    slice_recv,
    part_send,
    part_recv,
    send_sem,
    recv_sem,
    pass_sem,
    got_sem,
    side_send,
    side_recv,
):
    me, column = lax.axis_index("ep"), lax.axis_index("pd")
    here = lax.div(me, 2)
    chips = list(range(2, ep_size, 2))
    near = [mask for mask in chips if 2 * mask < ep_size]
    far = [mask for mask in chips if 2 * mask >= ep_size]
    latent_width = gain.shape[-1]
    meet_peers(ep_size, pd_size)

    def chip(mask):
        return lax.div(me ^ mask, 2)

    def outward(mask):
        return remote(
            slices.at[chip(mask)],
            arrived.at[here],
            slice_send.at[mask],
            slice_recv.at[mask],
            {"ep": me ^ mask},
        )

    def homeward(mask):
        return remote(
            partial.at[chip(mask)],
            returned.at[here],
            part_send.at[mask],
            part_recv.at[mask],
            {"ep": me ^ mask},
        )

    for mask in far[:1] + near:
        outward(mask).start()
    def weighed(rows):
        return jnp.dot(rows, weight[...], preferred_element_type=jnp.float32)

    for mask in chips:
        partial[chip(mask), token_rows:] = weighed(draft_slices[chip(mask)]).astype(jnp.bfloat16)
    total = jnp.concatenate([weighed(slices[here]), weighed(draft_slices[here])], axis=0)
    for at, mask in enumerate(far):
        outward(mask).wait_send()
        for later in far[at + 1 : at + 2]:
            outward(later).start()
        for ready in [mask] if at else near + [mask]:
            outward(ready).wait_recv()
            partial[chip(ready), :token_rows] = weighed(arrived[chip(ready)]).astype(jnp.bfloat16)
            homeward(ready).start()
    for mask in chips:
        homeward(mask).wait_recv()
        total = total + returned[chip(mask)].astype(jnp.float32)
    lead = total[:, :latent_width]
    scale = lax.rsqrt(jnp.mean(lead * lead, axis=-1, keepdims=True) + NORM_EPSILON)
    own_latent[:, :latent_width] = (lead * scale * gain[...]).astype(jnp.bfloat16)
    own_latent[:, latent_width:] = total[:, latent_width:].astype(jnp.bfloat16)
    mine = own_latent.at[pl.ds(0, token_rows)]

    def direct(mask):
        return remote(
            mine,
            out.at[column, me],
            send_sem.at[mask],
            recv_sem.at[mask],
            {"ep": me ^ mask},
        )

    def across(mask, step):
        return remote(
            mine if mask == 0 else out.at[column, me ^ mask],
            out.at[column, me ^ mask],
            pass_sem.at[step, mask],
            got_sem.at[step, mask],
            {"pd": lax.rem(column + step, pd_size)},
        )

    def beside(mask, step):
        origin = lax.rem(column - step + pd_size, pd_size)
        here = out.at[origin, me ^ mask]
        return remote(
            mine if mask == 0 and step == 0 else here,
            here,
            side_send.at[step, mask],
            side_recv.at[step, mask],
            {"ep": me ^ 1},
        )

    for step in range(1, pd_size):
        across(0, step).start()
    for mask in chips[::-1]:
        direct(mask).start()
    beside(0, 0).start()
    own = pltpu.make_async_copy(mine, out.at[column, me], local_sem)
    own.start()
    for mask in chips:
        direct(mask).wait_recv()
        for step in range(1, pd_size):
            across(mask, step).start()
        beside(mask, 0).start()
    for mask in [0] + chips:
        for step in range(1, pd_size):
            across(mask, step).wait_recv()
            beside(mask, step).start()
    own.wait()
    for mask in near:
        outward(mask).wait_send()
    for mask in chips:
        homeward(mask).wait_send()
        direct(mask).wait_send()
    for mask in [0] + chips:
        for step in range(pd_size):
            if step:
                across(mask, step).wait_send()
            beside(mask, step).wait()


def latents(slices, draft_slices, weight, gain, collective_id):
    ep_size, pd_size = lax.axis_size("ep"), lax.axis_size("pd")
    token_rows, width = slices.shape[1], weight.shape[1]
    rows = token_rows + draft_slices.shape[1]
    vmem = pl.BlockSpec(memory_space=pltpu.VMEM)
    dma = pltpu.SemaphoreType.DMA
    return pl.pallas_call(
        functools.partial(latent_kernel, ep_size, pd_size, token_rows),
        out_shape=(
            jax.ShapeDtypeStruct((pd_size, ep_size, token_rows, width), jnp.bfloat16),
            jax.ShapeDtypeStruct((rows, width), jnp.bfloat16),
        ),
        in_specs=[vmem] * 4,
        out_specs=(vmem, vmem),
        scratch_shapes=[
            pltpu.VMEM(slices.shape, jnp.bfloat16),
            pltpu.VMEM((ep_size // 2, rows, width), jnp.bfloat16),
            pltpu.VMEM((ep_size // 2, rows, width), jnp.bfloat16),
            dma,
            *([dma((ep_size,))] * 6),
            *([dma((pd_size, ep_size))] * 4),
        ],
        compiler_params=pltpu.CompilerParams(
            collective_id=collective_id, has_side_effects=True, vmem_limit_bytes=48 * 2**20
        ),
    )(slices, draft_slices, weight, gain)


def collect_kernel(
    ep_size,
    pd_size,
    pieces,
    window,
    partial_out,
    out,
    own_rows,
    other_rows,
    summed,
    own_sem,
    local_sem,
    pass_sem,
    got_sem,
    send_sem,
    recv_sem,
):
    me, column = lax.axis_index("ep"), lax.axis_index("pd")
    near, far = near_and_far(ep_size)
    width = out.shape[-1] // pieces
    items = [(mask, piece) for mask in far + near + [0] for piece in range(pieces)]
    meet_peers(ep_size, pd_size)

    def across(mask, piece, step):
        target = me ^ mask
        there = lax.rem(column + step, pd_size)
        columns = pl.ds(piece * width, width)
        return remote(
            partial_out.at[there, target, :, columns],
            other_rows.at[step - 1, target, :, columns],
            pass_sem.at[step, mask, piece],
            got_sem.at[step, mask, piece],
            {"pd": there},
        )

    def direct(mask, piece):
        columns = pl.ds(piece * width, width)
        return remote(
            summed.at[me ^ mask, :, columns],
            out.at[me, :, columns],
            send_sem.at[mask, piece],
            recv_sem.at[mask, piece],
            {"ep": me ^ mask},
        )

    for item in items[:window]:
        for step in range(1, pd_size):
            across(*item, step).start()
    fetch = pltpu.make_async_copy(partial_out.at[column], own_rows, own_sem)
    fetch.start()
    fetch.wait()
    for at, item in enumerate(items):
        mask, piece = item
        target = me ^ mask
        columns = pl.ds(piece * width, width)
        for step in range(1, pd_size):
            across(*item, step).wait()
            if at + window < len(items):
                across(*items[at + window], step).start()
        total = own_rows[target, :, columns].astype(jnp.float32)
        for step in range(1, pd_size):
            total = total + other_rows[step - 1, target, :, columns].astype(jnp.float32)
        summed[target, :, columns] = total.astype(jnp.bfloat16)
        if mask:
            direct(*item).start()
    keep = pltpu.make_async_copy(summed.at[me], out.at[me], local_sem)
    keep.start()
    for mask, piece in items:
        if mask:
            direct(mask, piece).wait()
    keep.wait()


def collect(partial_out, pieces, window, collective_id):
    pd_size, ep_size, capacity, width = partial_out.shape
    return pl.pallas_call(
        functools.partial(collect_kernel, ep_size, pd_size, pieces, window),
        out_shape=jax.ShapeDtypeStruct((ep_size, capacity, width), jnp.bfloat16),
        in_specs=[pl.BlockSpec(memory_space=pl.ANY)],
        out_specs=pl.BlockSpec(memory_space=pl.ANY),
        scratch_shapes=[
            pltpu.VMEM((ep_size, capacity, width), jnp.bfloat16),
            pltpu.VMEM((pd_size - 1, ep_size, capacity, width), jnp.bfloat16),
            pltpu.VMEM((ep_size, capacity, width), jnp.bfloat16),
            pltpu.SemaphoreType.DMA,
            pltpu.SemaphoreType.DMA,
            pltpu.SemaphoreType.DMA((pd_size, ep_size, pieces)),
            pltpu.SemaphoreType.DMA((pd_size, ep_size, pieces)),
            pltpu.SemaphoreType.DMA((ep_size, pieces)),
            pltpu.SemaphoreType.DMA((ep_size, pieces)),
        ],
        compiler_params=pltpu.CompilerParams(
            collective_id=collective_id, has_side_effects=True, vmem_limit_bytes=48 * 2**20
        ),
    )(partial_out)


def per_device(
    hidden,
    moe_gain,
    expert_ids,
    gate_scores,
    gate_up,
    down_proj,
    kv_weight,
    attn_gain,
    kv_gain,
    prompt_lens,
    assign,
    latent_cache,
    cache_len,
    draft_hidden,
    queries,
):
    tok_rows, model_width = hidden.shape
    top_count = expert_ids.shape[1]
    experts = lax.axis_size("ep")
    quarters = lax.axis_size("pd")
    capacity = max(2, 2 * tok_rows * top_count // experts)
    normed = rms_norm(hidden.astype(jnp.float32), moe_gain).astype(jnp.bfloat16)
    route_weight = ROUTE_SCALE * gate_scores / jnp.sum(gate_scores, axis=-1, keepdims=True)
    flat_ids = expert_ids.reshape(-1)
    one_hot = (flat_ids[:, None] == jnp.arange(experts, dtype=jnp.int32)[None, :]).astype(jnp.int32)
    slot_rank = jnp.sum(
        one_hot * (jnp.cumsum(one_hot, axis=0, dtype=jnp.int32) - 1), axis=1, dtype=jnp.int32
    )
    target = flat_ids * capacity + slot_rank
    hits = jnp.arange(experts * capacity, dtype=jnp.int32)[:, None, None] == target.reshape(
        1, tok_rows, top_count
    )
    select = jnp.any(hits, axis=-1).astype(jnp.bfloat16)
    mix = jnp.sum(jnp.where(hits, route_weight[None], 0.0), axis=-1)
    slot_count, step_count = (draft_hidden.shape[0], draft_hidden.shape[1])
    draft_rows = slot_count * step_count
    draft_input = rms_norm(
        draft_hidden.reshape(draft_rows, model_width).astype(jnp.float32), attn_gain
    ).astype(jnp.bfloat16)
    drafts = jnp.pad(draft_input, ((0, -draft_rows % 16), (0, 0)))
    drafts = drafts.reshape(-1, experts // 2, 2 * kv_weight.shape[0]).swapaxes(0, 1)
    gate_local = gate_up[0]
    down_local = down_proj[0]
    arrived, weight_pair, draft_slices = spread(
        select.reshape(experts, capacity, tok_rows), normed, kv_weight, drafts, 4, 4, 1
    )
    row_block = arrived.reshape(-1, model_width)
    gate_val = jnp.einsum("rd,dgf->rgf", row_block, gate_local, preferred_element_type=jnp.float32)
    partial_value = jnp.dot(
        (jax.nn.silu(gate_val[:, 0]) * gate_val[:, 1]).astype(jnp.bfloat16),
        down_local,
        preferred_element_type=jnp.float32,
    ).astype(jnp.bfloat16)
    partial_out = partial_value.reshape(arrived.shape)
    expert_out = collect(partial_out, 4, 6, 2).reshape(-1, model_width)
    mix_high = mix.astype(jnp.bfloat16)
    mix_low = (mix - mix_high.astype(jnp.float32)).astype(jnp.bfloat16)
    both = jnp.einsum(
        "asr,sd->ard",
        jnp.stack([mix_high, mix_low]),
        expert_out,
        preferred_element_type=jnp.float32,
    )
    mixture = both[0] + both[1]
    layer_out = (hidden.astype(jnp.float32) + mixture).astype(jnp.bfloat16)
    latent_width = kv_gain.shape[0]
    row_width = kv_weight.shape[1]
    kv_input = rms_norm(layer_out.astype(jnp.float32), attn_gain).astype(jnp.bfloat16)
    slices = kv_input.reshape(tok_rows, experts // 2, 2 * kv_weight.shape[0]).swapaxes(0, 1)
    shard_rows, own_latent = latents(
        slices, draft_slices, weight_pair.reshape(-1, row_width), kv_gain[None], 3
    )
    draft_latent = own_latent[tok_rows : tok_rows + slot_count * step_count].reshape(
        slot_count, step_count, row_width
    )
    device = lax.axis_index(("ep", "pd"))
    slot_ids = device * slot_count + jnp.arange(slot_count, dtype=jnp.int32)
    owner_hit = assign[None, :] == slot_ids[:, None]
    ends = jnp.cumsum(prompt_lens, dtype=jnp.int32)
    starts = ends - prompt_lens
    first_row = jnp.sum(jnp.where(owner_hit, starts[None, :], 0), axis=1, dtype=jnp.int32)
    block_len = jnp.sum(jnp.where(owner_hit, prompt_lens[None, :], 0), axis=1, dtype=jnp.int32)
    block_cap = 3 * tok_rows
    block_ids = jnp.arange(block_cap, dtype=jnp.int32)
    wanted = first_row[:, None] + block_ids[None, :]
    live_rows = block_ids[None, :] < block_len[:, None]
    shard_rows = shard_rows.reshape(-1, row_width)
    places = jnp.arange(quarters * experts * tok_rows, dtype=jnp.int32)
    from_pd, from_ep = places // (experts * tok_rows), places // tok_rows % experts
    row_index = (from_ep * quarters + from_pd) * tok_rows + places % tok_rows
    picker = ((row_index[None, None, :] == wanted[:, :, None]) & live_rows[:, :, None]).astype(
        jnp.bfloat16
    )
    blocks = jnp.einsum(
        "srn,nk->srk", picker, shard_rows, preferred_element_type=jnp.float32
    ).astype(jnp.bfloat16)
    decoded = jnp.stack(
        [
            slot_attention(
                queries[0],
                latent_cache[0],
                blocks[0],
                draft_latent[0],
                cache_len[0],
                block_len[0],
                latent_width,
            )
        ],
        axis=0,
    )
    return (layer_out, decoded)


def solution(mesh):
    in_specs = (
        P(("groups", "ep", "pd"), None),
        P(),
        P(("groups", "ep", "pd"), None),
        P(("groups", "ep", "pd"), None),
        P("ep", None, None, "pd"),
        P("ep", "pd", None),
        P("ep", None),
        P(),
        P(),
        P("groups"),
        P("groups"),
        P(("groups", "ep", "pd"), None, None),
        P(("groups", "ep", "pd")),
        P(("groups", "ep", "pd"), None, None),
        P(("groups", "ep", "pd"), None, None, None),
    )
    out_specs = (P(("groups", "ep", "pd"), None), P(("groups", "ep", "pd"), None, None, None))
    return jax.shard_map(
        per_device, mesh=mesh, in_specs=in_specs, out_specs=out_specs, check_vma=False
    )
```
